256 devices in a mesh: section: 2 (over core), seq: 8 (over z), chan: 16 (over y, x).
Axes of the slice: x: 4, y: 4, z: 8, core: 2. Of those that a mesh axis runs over, the one named last changes fastest.
Arguments:
- inputs: bfloat16 [2, 512, 4096], P(None, 'seq', 'chan'), may hold values from -8 to 8
- out_grad: bfloat16 [2, 512, 4096], P(None, 'seq', 'chan'), may hold values from -0.5 to 0.5
- short_filters: float32 [2, 3, 7, 4096], P('section', None, None, 'chan'), may hold values from -2 to 2
- long_filters: float32 [2, 128, 4096], P('section', None, 'chan'), may hold values from -0.5 to 0.5
- skip_gain: float32 [2, 4096], P('section', 'chan'), may hold values from -1 to 1
- norm_gain: float32 [2, 4096], P('section', 'chan'), may hold values from 0.5 to 1.5
Outputs:
- param_grads: float32 [2, 151, 4096], P('section', None, 'chan')
The draws below stay inside these ranges and needn't reach their ends.
All inputs are finite; a program needn't handle non-finite values.
Results may differ from the reference program's by a relative error of at most 0.012.
The reference program's roundings to bfloat16 on the way count: a program that leaves them out, or rounds other values in their place, can miss the bound.
Values may be sent and summed in bfloat16 or wider, within the bound.
No kernel may reach another device: no remote copies, remote signals or barrier semaphores. Data moves between devices by JAX's collectives and lax.ppermute only.
A program may use at most 64 MiB of HBM per device.

```python
import math
import jax
import jax.numpy as jnp
from jax import lax

D = 4096
KS = 7
KL = 128
MICRO = 2
LAYERS = 2
SEQ = 512


def draw_inputs(key, part):
    keys = jax.random.split(key, 3)
    columns = jnp.exp(jax.random.uniform(keys[1], (D,), jnp.float32, math.log(0.3), math.log(3.0)))
    base = jax.random.normal(keys[0], (MICRO, SEQ, D), jnp.float32)
    row_scales = jnp.exp(jax.random.uniform(keys[2], (MICRO, SEQ, 1), jnp.float32, math.log(0.5), math.log(2.0)))
    values = base * row_scales * columns
    return jnp.clip(values, -8.0, 8.0).astype(jnp.bfloat16)


def shard_levels(rng, extent, cuts, low, largest):
    factor_of = 1.0
    for axis_at, parts in cuts:
        heights = jax.random.uniform(jax.random.fold_in(jax.random.fold_in(rng, 6), axis_at), (parts,), jnp.float32, low / len(cuts), largest / len(cuts))
        factor_of = factor_of * jnp.repeat(jnp.exp(heights), extent[axis_at] // parts).reshape((-1,) + (1,) * (len(extent) - 1 - axis_at))
    return factor_of


def gaussian(rng, shape, scale, reach, cuts=(), held_as=jnp.bfloat16):
    array = scale * jax.random.normal(rng, shape, jnp.float32)
    if cuts:
        array = array * shard_levels(rng, shape, cuts, -0.22, 0.18)
    return jnp.clip(array, -reach, reach).astype(held_as)


def setup_inputs(seed: int = 0) -> dict:
    arg_keys = jax.random.split(jax.random.key(seed), 7)
    inputs = draw_inputs(jax.random.fold_in(arg_keys[6], 71), 0)
    out_grad = gaussian(arg_keys[1], (MICRO, SEQ, D), ((MICRO * SEQ) ** -0.5), 0.5, ((1, 8), (2, 16)))
    short_filters = gaussian(arg_keys[2], (LAYERS, 3, KS, D), KS ** -0.5, 2.0, ((0, 2), (3, 16)), jnp.float32)
    long_filters = gaussian(arg_keys[3], (LAYERS, KL, D), KL ** -0.5, 0.5, ((0, 2), (2, 16)), jnp.float32)
    skip_gain = jnp.clip(jax.random.uniform(arg_keys[4], (LAYERS, D), jnp.float32, -1.0, 1.0) * shard_levels(arg_keys[4], (LAYERS, D), ((0, 2), (1, 16)), -0.4, 0.0), -1.0, 1.0)
    norm_gain = jnp.clip(0.5 + 1.0 * jax.random.uniform(arg_keys[5], (LAYERS, D), jnp.float32) ** shard_levels(arg_keys[5], (LAYERS, D), ((0, 2), (1, 16)), -0.2, 0.2), 0.5, 1.5)
    return {"inputs": inputs, "out_grad": out_grad, "short_filters": short_filters, "long_filters": long_filters, "skip_gain": skip_gain, "norm_gain": norm_gain}


EPSILON = 1e-06

def causal(signal, filters):
    length = signal.shape[0]
    size = length + filters.shape[0]
    spectrum = jnp.fft.rfft(signal, size, axis=0) * jnp.fft.rfft(filters, size, axis=0)
    return jnp.fft.irfft(spectrum, size, axis=0)[:length]

def anticausal(signal, filters):
    return causal(signal[::-1], filters)[::-1]

def tap_sums(cotangent, signal, taps):
    length = signal.shape[0]
    size = 2 * length
    spectrum = jnp.fft.rfft(cotangent[::-1], size, axis=0) * jnp.fft.rfft(signal, size, axis=0)
    full = jnp.fft.irfft(spectrum, size, axis=0)[:length]
    return full[length - taps:][::-1]

def round_trip(values):
    return lax.optimization_barrier(values.astype(jnp.bfloat16)).astype(jnp.float32)

def layer_pieces(x_rows, shorts, longs, skip_row, gain_row):
    x_float = x_rows.astype(jnp.float32)
    scale = lax.rsqrt(lax.optimization_barrier(jnp.sum(x_float * x_float, axis=1)) / D + EPSILON)
    normed = round_trip(x_float * scale[:, None] * gain_row)
    query = causal(normed, shorts[0])
    key_rows = causal(normed, shorts[1])
    value_rows = causal(normed, shorts[2])
    mixed = round_trip(key_rows * value_rows)
    filtered = causal(mixed, longs) + skip_row * mixed
    return (x_float, scale, normed, query, key_rows, value_rows, mixed, filtered)

def reference(inputs, out_grad, short_filters, long_filters, skip_gain, norm_gain):
    layer_count = short_filters.shape[0]
    grad_list = [jnp.zeros((3 * KS + KL + 2, D), jnp.float32) for layer in range(layer_count)]
    for micro in range(MICRO):
        x_rows = inputs[micro]
        saved = []
        for layer in range(layer_count):
            saved.append(x_rows)
            pieces = layer_pieces(x_rows, short_filters[layer], long_filters[layer], skip_gain[layer], norm_gain[layer])
            x_rows = (pieces[0] + pieces[3] * pieces[7]).astype(jnp.bfloat16)
        cotangent = out_grad[micro]
        for layer in range(layer_count - 1, -1, -1):
            shorts = short_filters[layer]
            gain_row = norm_gain[layer]
            skip_row = skip_gain[layer]
            x_float, scale, normed, query, key_rows, value_rows, mixed, filtered = layer_pieces(saved[layer], shorts, long_filters[layer], skip_row, gain_row)
            e_float = cotangent.astype(jnp.float32)
            d_query = round_trip(e_float * filtered)
            d_filtered = round_trip(e_float * query)
            d_mixed = anticausal(d_filtered, long_filters[layer]) + skip_row * d_filtered
            d_key = round_trip(d_mixed * value_rows)
            d_value = round_trip(d_mixed * key_rows)
            d_normed = anticausal(d_query, shorts[0]) + anticausal(d_key, shorts[1]) + anticausal(d_value, shorts[2])
            fresh = jnp.concatenate([tap_sums(d_query, normed, KS), tap_sums(d_key, normed, KS), tap_sums(d_value, normed, KS), tap_sums(d_filtered, mixed, KL), lax.optimization_barrier(jnp.sum(d_filtered * mixed, axis=0))[None], lax.optimization_barrier(jnp.sum(d_normed * x_float * scale[:, None], axis=0))[None]], axis=0)
            grad_list[layer] = grad_list[layer] + fresh
            norm_term = lax.optimization_barrier(jnp.sum(gain_row * d_normed * x_float, axis=1)) / D
            cotangent = (e_float + scale[:, None] * gain_row * d_normed - x_float * (scale * scale * scale)[:, None] * norm_term[:, None]).astype(jnp.bfloat16)
    return jnp.stack(grad_list, axis=0)
```

```python
import functools

import jax
import jax.numpy as jnp
from jax import lax
from jax.experimental import pallas as pl
from jax.experimental.pallas import tpu as pltpu
from jax.sharding import PartitionSpec as P

EPSILON = 1e-06
SHARDS = 8
ROWS = 64
LANES = 128
KS = 7
KL = 128
PARAMS = 152
SHORT_AT, SKIP_AT, GAIN_AT = 128, 149, 150
QUARTER = ROWS // 4
MESSAGE = 64
f32 = jnp.float32
bf16 = jnp.bfloat16


def rounded(a):
    return a.astype(bf16).astype(f32)


def later(a, count):
    sub = lax.broadcasted_iota(jnp.int32, a.shape, 1)
    return jnp.where(sub >= count, pltpu.roll(a, count, 1), 0.0)


def sooner(a, count):
    sub = lax.broadcasted_iota(jnp.int32, a.shape, 1)
    return jnp.where(sub < SHARDS - count, pltpu.roll(a, SHARDS - count, 1), 0.0)


def eye():
    shape = (LANES, LANES)
    return lax.broadcasted_iota(jnp.int32, shape, 0) == lax.broadcasted_iota(jnp.int32, shape, 1)


def send_sums(out_ref, chunk_of):
    diagonal = eye()
    rows = []
    for b in range(4):
        column = jnp.sum(chunk_of(b), axis=1, keepdims=True)
        rows.append(jnp.sum(jnp.where(diagonal, column, 0.0), axis=0, keepdims=True))
    whole = jnp.concatenate(rows, axis=0)
    out_ref[...] = jnp.broadcast_to(whole[None], out_ref.shape)


def column_of(row, diagonal):
    column = jnp.sum(jnp.where(diagonal, row, 0.0), axis=1, keepdims=True)
    return jnp.broadcast_to(column, (LANES, LANES)).reshape(16, SHARDS, LANES)


def spread(p_ref, taps):
    @pl.loop(0, PARAMS // 8)
    def _(g):
        rows = p_ref[pl.ds(pl.multiple_of(g * 8, 8), 8), :]
        for k in range(8):
            taps[g * 8 + k] = jnp.broadcast_to(rows[k : k + 1], (8, LANES))


def scale_and_norm(width, x_ref, sums_ref, taps, scale_ref, normed):
    total = jnp.sum(sums_ref[...], axis=0)
    scale_rows = lax.rsqrt(total * (1.0 / width) + EPSILON)
    diagonal = eye()
    gain = taps[GAIN_AT]
    for b in range(4):
        at = pl.ds(16 * b, 16)
        scale = column_of(scale_rows[b : b + 1], diagonal)
        scale_ref[at] = scale
        normed[pl.ds(8 + 16 * b, 16)] = rounded(x_ref[at] * scale * gain[None])
    normed[pl.ds(0, 8)] = later(normed[pl.ds(64, 8)], 1)


def forward(taps, normed, mixed, q_ref, k_ref, v_ref, f_ref):
    @pl.loop(0, ROWS // 8)
    def _(b):
        near = normed[pl.ds(b * 8, 16)]
        streams = []
        for i in range(3):
            total = None
            for j in range(KS):
                term = taps[SHORT_AT + KS * i + j][None] * near[8 - j : 16 - j]
                total = term if total is None else total + term
            streams.append(total)
        at = pl.ds(b * 8, 8)
        q_ref[at] = streams[0]
        k_ref[at] = streams[1]
        v_ref[at] = streams[2]
        z = rounded(streams[1] * streams[2])
        mixed[pl.ds(128 + b * 8, 8)] = z
        mixed[pl.ds(64 + b * 8, 8)] = later(z, 1)
        mixed[pl.ds(b * 8, 8)] = later(z, 2)

    skip = taps[SKIP_AT]

    @pl.loop(0, ROWS // 16)
    def _(b):
        def step(g, total):
            z = mixed[pl.ds(113 + 16 * b - 16 * g, 31)]
            w = taps[pl.ds(16 * g, 16)]
            for a in range(16):
                total = total + w[a][None] * z[15 - a : 31 - a]
            return total

        own = mixed[pl.ds(128 + 16 * b, 16)]
        f_ref[pl.ds(16 * b, 16)] = lax.fori_loop(0, KL // 16, step, skip[None] * own)


def extend_after(ref, whole):
    last = ref.shape[0] // 8 - 8
    if whole:

        @pl.loop(0, last)
        def _(b):
            a = ref[pl.ds((b % 8) * 8, 8)]
            shards = b // 8 + 1
            moved = jnp.where(shards == 1, sooner(a, 1), jnp.where(shards == 2, sooner(a, 2), sooner(a, 3)))
            ref[pl.ds(64 + b * 8, 8)] = moved
    else:
        ref[pl.ds(64, 8)] = sooner(ref[pl.ds(0, 8)], 1)


def mixed_cotangent(taps, after, start, count):
    skip = taps[SKIP_AT]

    def step(g, total):
        z = after[pl.ds(start + 16 * g, count + 15)]
        w = taps[pl.ds(16 * g, 16)]
        for a in range(16):
            total = total + w[a][None] * z[a : a + count]
        return total

    return lax.fori_loop(0, KL // 16, step, skip[None] * after[pl.ds(start, count)])


def normed_cotangent(taps, streams, start):
    total = None
    for i in range(3):
        near = streams[i][pl.ds(start, 16)]
        for j in range(KS):
            term = taps[SHORT_AT + KS * i + j][None] * near[j : j + 8]
            total = term if total is None else total + term
    return total


def over_shards(a):
    return jnp.sum(a, axis=1)


def gradients(out_ref, q, streams, normed, after, mixed, gain_term):
    start = q * QUARTER
    rows = []
    near = normed[pl.ds(start, QUARTER + 8)]
    for i in range(3):
        stream = streams[i][pl.ds(start, QUARTER)]
        for j in range(KS):
            rows.append(jnp.sum(stream * near[8 - j : 8 - j + QUARTER], axis=0))
    rows.append(jnp.sum(after[pl.ds(start, QUARTER)] * mixed[pl.ds(128 + start, QUARTER)], axis=0))
    rows.append(gain_term)
    while len(rows) < 32:
        rows.append(jnp.zeros((SHARDS, LANES), f32))
    out_ref[pl.ds(0, 32), :] = over_shards(jnp.stack(rows, axis=0))
    for half in range(2):
        first = q * 32 + half * 16

        def step(b, total):
            d = after[pl.ds(b * 16, 16)]
            z = mixed[pl.ds(113 + b * 16 - first, 31)]
            new = []
            for a in range(16):
                new.append(total[a] + jnp.sum(d * z[15 - a : 31 - a], axis=0))
            return jnp.stack(new, axis=0)

        sums = lax.fori_loop(0, ROWS // 16, step, jnp.zeros((16, SHARDS, LANES), f32))
        out_ref[pl.ds(32 + half * 16, 16), :] = over_shards(sums)


def pack_kernel(where_ref, x_ref, g_ref, short_ref, long_ref, skip_ref, gain_ref, out_ref, own_ref, send_ref):
    section = where_ref[0]
    mine = pl.ds(pl.multiple_of(section * LANES, LANES), LANES)
    other = pl.ds(pl.multiple_of((1 - section) * LANES, LANES), LANES)
    for z in range(SHARDS):
        out_ref[z, pl.ds(0, ROWS), :] = x_ref[z % 2, :, mine]
        out_ref[z, pl.ds(ROWS, ROWS), :] = g_ref[z % 2, :, mine]
    for ref, half in ((own_ref, mine), (send_ref, other)):
        ref[pl.ds(0, KL), :] = long_ref[0, :, half]
        for i in range(3):
            ref[pl.ds(SHORT_AT + KS * i, KS), :] = short_ref[0, i, :, half]
        ref[pl.ds(SKIP_AT, 1), :] = skip_ref[:, half]
        ref[pl.ds(GAIN_AT, 1), :] = gain_ref[:, half]
        ref[pl.ds(PARAMS - 1, 1), :] = jnp.zeros((1, LANES), f32)


def open_kernel(where_ref, in_ref, own_ref, other_ref, x_ref, g_ref, p0_ref, p1_ref, out_ref, wide):
    section = where_ref[0]
    for part, ref in enumerate((x_ref, g_ref)):
        for z in range(SHARDS):
            wide[part, pl.ds(z * ROWS, ROWS), :] = in_ref[z, pl.ds(part * ROWS, ROWS), :].astype(f32)
        for v in range(ROWS):
            ref[v] = wide[part, pl.ds(v, SHARDS, stride=ROWS), :]
    own = own_ref[...]
    other = other_ref[...]
    p0_ref[...] = jnp.where(section == 0, own, other)
    p1_ref[...] = jnp.where(section == 0, other, own)

    def chunk(b):
        x = x_ref[pl.ds(16 * b, 16)].reshape(LANES, LANES)
        return x * x

    send_sums(out_ref, chunk)


def first_kernel(
    width, x_ref, sums_ref, p_ref, x1_ref, q_ref, k_ref, v_ref, f_ref, mixed_ref, normed_ref, scale_ref, out_ref, taps
):
    spread(p_ref, taps)
    scale_and_norm(width, x_ref, sums_ref, taps, scale_ref, normed_ref)
    forward(taps, normed_ref, mixed_ref, q_ref, k_ref, v_ref, f_ref)

    def chunk(b):
        at = pl.ds(16 * b, 16)
        x1 = rounded(x_ref[at] + q_ref[at] * f_ref[at])
        x1_ref[at] = x1
        return (x1 * x1).reshape(LANES, LANES)

    send_sums(out_ref, chunk)


def second_kernel(
    width, where_ref, x_ref, g_ref, sums_ref, p_ref, d_ref, scale_ref, grads_ref, out_ref,
    taps, normed, mixed, q_ref, k_ref, v_ref, f_ref, after, sq, sk, sv
):
    q = where_ref[1]
    spread(p_ref, taps)
    scale_and_norm(width, x_ref, sums_ref, taps, scale_ref, normed)
    forward(taps, normed, mixed, q_ref, k_ref, v_ref, f_ref)

    @pl.loop(0, ROWS // 8)
    def _(b):
        at = pl.ds(b * 8, 8)
        e = g_ref[at]
        sq[at] = rounded(e * f_ref[at])
        after[at] = rounded(e * q_ref[at])

    extend_after(after, True)

    @pl.loop(0, ROWS // 16)
    def _(b):
        at = pl.ds(b * 16, 16)
        d_mixed = mixed_cotangent(taps, after, b * 16, 16)
        sk[at] = rounded(d_mixed * v_ref[at])
        sv[at] = rounded(d_mixed * k_ref[at])

    for ref in (sq, sk, sv):
        extend_after(ref, False)

    @pl.loop(0, ROWS // 8)
    def _(b):
        d_ref[pl.ds(b * 8, 8)] = normed_cotangent(taps, (sq, sk, sv), b * 8)

    gain = taps[GAIN_AT]

    def chunk(b):
        at = pl.ds(16 * b, 16)
        return (gain[None] * d_ref[at] * x_ref[at]).reshape(LANES, LANES)

    send_sums(out_ref, chunk)
    at = pl.ds(q * QUARTER, QUARTER)
    gain_term = jnp.sum(d_ref[at] * x_ref[at] * scale_ref[at], axis=0)
    gradients(grads_ref, q, (sq, sk, sv), normed, after, mixed, gain_term)


def third_kernel(
    width, where_ref, x_ref, x1_ref, g_ref, d1_ref, scale1_ref, sums_ref, p0_ref, p1_ref,
    scale_ref, normed, mixed, q_ref, k_ref, v_ref, f_ref, grads1_ref, out_ref,
    taps, after, sq, sk, sv, kx, vx, grads
):
    q = where_ref[1]
    spread(p0_ref, taps)
    total = jnp.sum(sums_ref[...], axis=0) * (1.0 / width)
    diagonal = eye()
    gain1 = jnp.broadcast_to(p1_ref[pl.ds(GAIN_AT, 1), :], (8, LANES))[None]
    for b in range(4):
        at = pl.ds(16 * b, 16)
        term = column_of(total[b : b + 1], diagonal)
        scale = scale1_ref[at]
        e = rounded(g_ref[at] + scale * gain1 * d1_ref[at] - x1_ref[at] * (scale * scale * scale) * term)
        sq[at] = rounded(e * f_ref[at])
        after[at] = rounded(e * q_ref[at])
        kx[at] = k_ref[at]
        vx[at] = v_ref[at]
    extend_after(after, True)
    for ref in (sq, kx, vx):
        extend_after(ref, False)
    start = q * QUARTER

    for part in range(2):
        at = pl.ds(start + 12 * part, 12)
        d_mixed = mixed_cotangent(taps, after, start + 12 * part, 12)
        sk[at] = rounded(d_mixed * vx[at])
        sv[at] = rounded(d_mixed * kx[at])

    gain_term = jnp.zeros((SHARDS, LANES), f32)
    for b in range(2):
        at = pl.ds(start + 8 * b, 8)
        d_normed = normed_cotangent(taps, (sq, sk, sv), start + 8 * b)
        gain_term = gain_term + jnp.sum(d_normed * x_ref[at] * scale_ref[at], axis=0)
    gradients(grads, q, (sq, sk, sv), normed, after, mixed, gain_term)
    message0 = grads[...].astype(bf16)
    message1 = grads1_ref[...].astype(bf16)
    for z in range(SHARDS):
        out_ref[z] = message0
        out_ref[SHARDS + z] = message1


def close_kernel(in_ref, out_ref):
    for half in range(2):
        lanes = pl.ds(half * LANES, LANES)
        sums = None
        for q in range(4):
            pair = in_ref[half * SHARDS + 2 * q].astype(f32) + in_ref[half * SHARDS + 2 * q + 1].astype(f32)
            out_ref[0, pl.ds(3 * KS + 32 * q, 32), lanes] = pair[32:]
            sums = pair[:32] if sums is None else sums + pair[:32]
        out_ref[0, pl.ds(0, 3 * KS), lanes] = sums[: 3 * KS]
        out_ref[0, pl.ds(3 * KS + KL, 2), lanes] = sums[3 * KS : 3 * KS + 2]


VMEM = pl.BlockSpec(memory_space=pltpu.VMEM)
SMEM = pl.BlockSpec(memory_space=pltpu.SMEM)


def call(kernel, name, outs, operands, scratch=(), scalars=0):
    return pl.pallas_call(
        kernel,
        name=name,
        out_shape=[jax.ShapeDtypeStruct(shape, dtype) for shape, dtype in outs],
        in_specs=[SMEM] * scalars + [VMEM] * (len(operands) - scalars),
        out_specs=[VMEM] * len(outs),
        scratch_shapes=[pltpu.VMEM(shape, dtype) for shape, dtype in scratch],
        compiler_params=pltpu.CompilerParams(vmem_limit_bytes=40 * 1024 * 1024),
    )(*operands)


def block(rows):
    return ((rows, SHARDS, LANES), f32)


def on_device(inputs, out_grad, short_filters, long_filters, skip_gain, norm_gain):
    chan = lax.axis_size("chan")
    width = chan * inputs.shape[2]
    group = 2 * chan
    where = jnp.stack([lax.axis_index("section"), lax.axis_index("seq") // 2]).astype(jnp.int32)
    params = ((PARAMS, LANES), f32)
    sums = ((group, 4, LANES), f32)

    packed, own, send = call(
        pack_kernel,
        "pack",
        [((SHARDS, 2 * ROWS, LANES), bf16), params, params],
        (where, inputs, out_grad, short_filters, long_filters, skip_gain, norm_gain),
        scalars=1,
    )
    other = lax.ppermute(send, "section", [(0, 1), (1, 0)])
    arrived = lax.all_to_all(packed, "seq", 0, 0)
    x0, g, p0, p1, part = call(
        open_kernel,
        "open",
        [block(ROWS), block(ROWS), params, params, sums],
        (where, arrived, own, other),
        [((2, SHARDS * ROWS, LANES), f32)],
        scalars=1,
    )

    def over_channels(part):
        return lax.all_to_all(part, ("section", "chan"), 0, 0)

    x1, q0, k0, v0, f0, mixed0, normed0, scale0, part = call(
        functools.partial(first_kernel, width),
        "first",
        [block(ROWS)] * 5 + [block(192), block(ROWS + 8), block(ROWS), sums],
        (x0, over_channels(part), p0),
        [block(PARAMS)],
    )
    d1, scale1, grads1, part = call(
        functools.partial(second_kernel, width),
        "second",
        [block(ROWS), block(ROWS), ((MESSAGE, LANES), f32), sums],
        (where, x1, g, over_channels(part), p1),
        [block(PARAMS), block(ROWS + 8), block(192)] + [block(ROWS)] * 4 + [block(192)] + [block(ROWS + 8)] * 3,
        scalars=1,
    )
    (message,) = call(
        functools.partial(third_kernel, width),
        "third",
        [((2 * SHARDS, MESSAGE, LANES), bf16)],
        (where, x0, x1, g, d1, scale1, over_channels(part), p0, p1, scale0, normed0, mixed0, q0, k0, v0, f0, grads1),
        [block(PARAMS), block(200)] + [block(ROWS + 8)] * 5 + [((MESSAGE, LANES), f32)],
        scalars=1,
    )
    gathered = lax.all_to_all(message, ("section", "seq"), 0, 0)
    (grads,) = call(
        close_kernel, "close", [((1, 3 * KS + KL + 2, 2 * LANES), f32)], (gathered,)
    )
    return grads


def solution(mesh):
    placed = (
        P(None, "seq", "chan"),
        P(None, "seq", "chan"),
        P("section", None, None, "chan"),
        P("section", None, "chan"),
        P("section", "chan"),
        P("section", "chan"),
    )
    return jax.shard_map(
        on_device, mesh=mesh, in_specs=placed, out_specs=P("section", None, "chan"), check_vma=False
    )
```

```python
import functools

import jax
import jax.numpy as jnp
from jax import lax
from jax.experimental import pallas as pl
from jax.experimental.pallas import tpu as pltpu
from jax.sharding import PartitionSpec as P

EPSILON = 1e-06
SHARDS = 8
ROWS = 64
LANES = 128
KS = 7
KL = 128
PARAMS = 152
SHORT_AT, SKIP_AT, GAIN_AT = 128, 149, 150
QUARTER = ROWS // 4
MESSAGE = 64
f32 = jnp.float32
bf16 = jnp.bfloat16


def rounded(a):
    return a.astype(bf16).astype(f32)


def later(a, count):
    sub = lax.broadcasted_iota(jnp.int32, a.shape, 1)
    return jnp.where(sub >= count, pltpu.roll(a, count, 1), 0.0)


def sooner(a, count):
    sub = lax.broadcasted_iota(jnp.int32, a.shape, 1)
    return jnp.where(sub < SHARDS - count, pltpu.roll(a, SHARDS - count, 1), 0.0)


def eye():
    shape = (LANES, LANES)
    return lax.broadcasted_iota(jnp.int32, shape, 0) == lax.broadcasted_iota(jnp.int32, shape, 1)


def send_sums(out_ref, chunk_of):
    diagonal = eye()
    rows = []
    for b in range(4):
        column = jnp.sum(chunk_of(b), axis=1, keepdims=True)
        rows.append(jnp.sum(jnp.where(diagonal, column, 0.0), axis=0, keepdims=True))
    whole = jnp.concatenate(rows, axis=0)
    out_ref[...] = jnp.broadcast_to(whole[None], out_ref.shape)


def column_of(row, diagonal):
    column = jnp.sum(jnp.where(diagonal, row, 0.0), axis=1, keepdims=True)
    return jnp.broadcast_to(column, (LANES, LANES)).reshape(16, SHARDS, LANES)


def scale_and_norm(width, x_ref, sums_ref, taps, scale_ref, normed):
    total = jnp.sum(sums_ref[...], axis=0)
    scale_rows = lax.rsqrt(total * (1.0 / width) + EPSILON)
    diagonal = eye()
    gain = taps[GAIN_AT]
    for b in range(4):
        at = pl.ds(16 * b, 16)
        scale = column_of(scale_rows[b : b + 1], diagonal)
        scale_ref[at] = scale
        normed[pl.ds(8 + 16 * b, 16)] = rounded(x_ref[at] * scale * gain[None])
    normed[pl.ds(0, 8)] = later(normed[pl.ds(64, 8)], 1)


def forward(taps, normed, mixed, q_ref, k_ref, v_ref, f_ref):
    @pl.loop(0, ROWS // 8)
    def _(b):
        near = normed[pl.ds(b * 8, 16)]
        streams = []
        for i in range(3):
            total = None
            for j in range(KS):
                term = taps[SHORT_AT + KS * i + j][None] * near[8 - j : 16 - j]
                total = term if total is None else total + term
            streams.append(total)
        at = pl.ds(b * 8, 8)
        q_ref[at] = streams[0]
        k_ref[at] = streams[1]
        v_ref[at] = streams[2]
        z = rounded(streams[1] * streams[2])
        mixed[pl.ds(128 + b * 8, 8)] = z
        mixed[pl.ds(64 + b * 8, 8)] = later(z, 1)
        mixed[pl.ds(b * 8, 8)] = later(z, 2)

    skip = taps[SKIP_AT]

    @pl.loop(0, ROWS // 16)
    def _(b):
        def step(g, total):
            z = mixed[pl.ds(113 + 16 * b - 16 * g, 31)]
            w = taps[pl.ds(16 * g, 16)]
            for a in range(16):
                total = total + w[a][None] * z[15 - a : 31 - a]
            return total

        own = mixed[pl.ds(128 + 16 * b, 16)]
        f_ref[pl.ds(16 * b, 16)] = lax.fori_loop(0, KL // 16, step, skip[None] * own)


def extend_after(ref, whole):
    last = ref.shape[0] // 8 - 8
    if whole:

        @pl.loop(0, last)
        def _(b):
            a = ref[pl.ds((b % 8) * 8, 8)]
            shards = b // 8 + 1
            moved = jnp.where(shards == 1, sooner(a, 1), jnp.where(shards == 2, sooner(a, 2), sooner(a, 3)))
            ref[pl.ds(64 + b * 8, 8)] = moved
    else:
        ref[pl.ds(64, 8)] = sooner(ref[pl.ds(0, 8)], 1)


def mixed_cotangent(taps, after, start, count):
    skip = taps[SKIP_AT]

    def step(g, total):
        z = after[pl.ds(start + 16 * g, count + 15)]
        w = taps[pl.ds(16 * g, 16)]
        for a in range(16):
            total = total + w[a][None] * z[a : a + count]
        return total

    return lax.fori_loop(0, KL // 16, step, skip[None] * after[pl.ds(start, count)])


def normed_cotangent(taps, streams, start):
    total = None
    for i in range(3):
        near = streams[i][pl.ds(start, 16)]
        for j in range(KS):
            term = taps[SHORT_AT + KS * i + j][None] * near[j : j + 8]
            total = term if total is None else total + term
    return total


def over_shards(a):
    return jnp.sum(a, axis=1)


def gradients(out_ref, q, streams, normed, after, mixed, gain_term):
    start = q * QUARTER
    rows = []
    near = normed[pl.ds(start, QUARTER + 8)]
    for i in range(3):
        stream = streams[i][pl.ds(start, QUARTER)]
        for j in range(KS):
            rows.append(jnp.sum(stream * near[8 - j : 8 - j + QUARTER], axis=0))
    rows.append(jnp.sum(after[pl.ds(start, QUARTER)] * mixed[pl.ds(128 + start, QUARTER)], axis=0))
    rows.append(gain_term)
    while len(rows) < 32:
        rows.append(jnp.zeros((SHARDS, LANES), f32))
    out_ref[pl.ds(0, 32), :] = over_shards(jnp.stack(rows, axis=0))
    for half in range(2):
        first = q * 32 + half * 16

        def step(b, total):
            d = after[pl.ds(b * 16, 16)]
            z = mixed[pl.ds(113 + b * 16 - first, 31)]
            new = []
            for a in range(16):
                new.append(total[a] + jnp.sum(d * z[15 - a : 31 - a], axis=0))
            return jnp.stack(new, axis=0)

        sums = lax.fori_loop(0, ROWS // 16, step, jnp.zeros((16, SHARDS, LANES), f32))
        out_ref[pl.ds(32 + half * 16, 16), :] = over_shards(sums)


def pack_kernel(x_ref, g_ref, out_ref, sems):
    mine = pl.ds(pl.multiple_of(lax.axis_index("section") * LANES, LANES), LANES)
    copies = []
    for z in range(SHARDS):
        for part, ref in enumerate((x_ref, g_ref)):
            target = out_ref.at[z, pl.ds(part * ROWS, ROWS), :]
            copies.append(pltpu.make_async_copy(ref.at[z % 2, :, mine], target, sems.at[2 * z + part]))
    for copy in copies:
        copy.start()
    for copy in copies:
        copy.wait()


def halves_kernel(short_ref, long_ref, skip_ref, gain_ref, own_ref, send_ref):
    section = lax.axis_index("section")
    mine = pl.ds(pl.multiple_of(section * LANES, LANES), LANES)
    other = pl.ds(pl.multiple_of((1 - section) * LANES, LANES), LANES)
    for ref, half in ((own_ref, mine), (send_ref, other)):
        ref[pl.ds(0, KL), :] = long_ref[0, :, half]
        for i in range(3):
            ref[pl.ds(SHORT_AT + KS * i, KS), :] = short_ref[0, i, :, half]
        ref[pl.ds(SKIP_AT, 1), :] = skip_ref[:, half]
        ref[pl.ds(GAIN_AT, 1), :] = gain_ref[:, half]
        ref[pl.ds(PARAMS - 1, 1), :] = jnp.zeros((1, LANES), f32)


def spread_kernel(own_ref, other_ref, taps0_ref, taps1_ref):
    first = lax.axis_index("section") == 0

    @pl.loop(0, PARAMS // 8)
    def _(g):
        at = pl.ds(pl.multiple_of(g * 8, 8), 8)
        own = own_ref[at, :]
        other = other_ref[at, :]
        for ref, rows in ((taps0_ref, jnp.where(first, own, other)), (taps1_ref, jnp.where(first, other, own))):
            for k in range(8):
                ref[g * 8 + k] = jnp.broadcast_to(rows[k : k + 1], (8, LANES))


def open_kernel(in_ref, x_ref, out_ref, wide):
    unpack(in_ref, 0, wide, x_ref)

    def chunk(b):
        x = x_ref[pl.ds(16 * b, 16)].reshape(LANES, LANES)
        return x * x

    send_sums(out_ref, chunk)


def unpack(in_ref, part, wide, ref):
    for z in range(SHARDS):
        wide[pl.ds(z * ROWS, ROWS), :] = in_ref[z, pl.ds(part * ROWS, ROWS), :].astype(f32)
    for v in range(ROWS):
        ref[v] = wide[pl.ds(v, SHARDS, stride=ROWS), :]


def cotangent_kernel(in_ref, g_ref, wide):
    unpack(in_ref, 1, wide, g_ref)


def first_kernel(
    width, x_ref, sums_ref, taps, x1_ref, q_ref, k_ref, v_ref, f_ref, mixed_ref, normed_ref, scale_ref, out_ref
):
    scale_and_norm(width, x_ref, sums_ref, taps, scale_ref, normed_ref)
    forward(taps, normed_ref, mixed_ref, q_ref, k_ref, v_ref, f_ref)

    def chunk(b):
        at = pl.ds(16 * b, 16)
        x1 = rounded(x_ref[at] + q_ref[at] * f_ref[at])
        x1_ref[at] = x1
        return (x1 * x1).reshape(LANES, LANES)

    send_sums(out_ref, chunk)


def second_kernel(
    width, x_ref, g_ref, sums_ref, taps,
    d_ref, scale_ref, normed, mixed, after, sq, sk, sv, out_ref,
    q_ref, k_ref, v_ref, f_ref
):
    scale_and_norm(width, x_ref, sums_ref, taps, scale_ref, normed)
    forward(taps, normed, mixed, q_ref, k_ref, v_ref, f_ref)

    @pl.loop(0, ROWS // 8)
    def _(b):
        at = pl.ds(b * 8, 8)
        e = g_ref[at]
        sq[at] = rounded(e * f_ref[at])
        after[at] = rounded(e * q_ref[at])

    extend_after(after, True)

    @pl.loop(0, ROWS // 16)
    def _(b):
        at = pl.ds(b * 16, 16)
        d_mixed = mixed_cotangent(taps, after, b * 16, 16)
        sk[at] = rounded(d_mixed * v_ref[at])
        sv[at] = rounded(d_mixed * k_ref[at])

    for ref in (sq, sk, sv):
        extend_after(ref, False)

    @pl.loop(0, ROWS // 8)
    def _(b):
        d_ref[pl.ds(b * 8, 8)] = normed_cotangent(taps, (sq, sk, sv), b * 8)

    gain = taps[GAIN_AT]

    def chunk(b):
        at = pl.ds(16 * b, 16)
        return (gain[None] * d_ref[at] * x_ref[at]).reshape(LANES, LANES)

    send_sums(out_ref, chunk)


def aside_kernel(
    width, x_ref, g_ref, d_ref, scale_ref, normed, mixed, after, sq, sk, sv, taps, k_ref, v_ref,
    grads_ref, base_ref, slope_ref, kx, vx
):
    q = lax.axis_index("seq") // 2
    at = pl.ds(q * QUARTER, QUARTER)
    gain_term = jnp.sum(d_ref[at] * x_ref[at] * scale_ref[at], axis=0)
    gradients(grads_ref, q, (sq, sk, sv), normed, after, mixed, gain_term)
    gain = taps[GAIN_AT][None]

    @pl.loop(0, ROWS // 8)
    def _(b):
        at = pl.ds(b * 8, 8)
        scale = scale_ref[at]
        base_ref[at] = g_ref[at] + scale * gain * d_ref[at]
        slope_ref[at] = x_ref[at] * (scale * scale * scale) * (1.0 / width)
        kx[at] = k_ref[at]
        vx[at] = v_ref[at]

    for ref in (kx, vx):
        extend_after(ref, False)


def third_kernel(
    base_ref, slope_ref, sums_ref, taps, x_ref, scale_ref, normed, mixed, q_ref, f_ref, kx, vx, grads1_ref,
    out_ref, after, sq, sk, sv, grads
):
    q = lax.axis_index("seq") // 2
    total = jnp.sum(sums_ref[...], axis=0)
    diagonal = eye()
    for b in range(4):
        at = pl.ds(16 * b, 16)
        e = rounded(base_ref[at] - slope_ref[at] * column_of(total[b : b + 1], diagonal))
        sq[at] = rounded(e * f_ref[at])
        after[at] = rounded(e * q_ref[at])
    extend_after(after, True)
    extend_after(sq, False)
    start = q * QUARTER

    for part in range(2):
        at = pl.ds(start + 12 * part, 12)
        d_mixed = mixed_cotangent(taps, after, start + 12 * part, 12)
        sk[at] = rounded(d_mixed * vx[at])
        sv[at] = rounded(d_mixed * kx[at])

    gain_term = jnp.zeros((SHARDS, LANES), f32)
    for b in range(2):
        at = pl.ds(start + 8 * b, 8)
        d_normed = normed_cotangent(taps, (sq, sk, sv), start + 8 * b)
        gain_term = gain_term + jnp.sum(d_normed * x_ref[at] * scale_ref[at], axis=0)
    gradients(grads, q, (sq, sk, sv), normed, after, mixed, gain_term)
    message0 = grads[...].astype(bf16)
    message1 = grads1_ref[...].astype(bf16)
    for z in range(SHARDS):
        out_ref[z] = message0
        out_ref[SHARDS + z] = message1


def close_kernel(in_ref, out_ref, whole, sem):
    for half in range(2):
        lanes = pl.ds(half * LANES, LANES)
        sums = None
        for q in range(4):
            pair = in_ref[half * SHARDS + 2 * q].astype(f32) + in_ref[half * SHARDS + 2 * q + 1].astype(f32)
            whole[0, pl.ds(3 * KS + 32 * q, 32), lanes] = pair[32:]
            sums = pair[:32] if sums is None else sums + pair[:32]
        whole[0, pl.ds(0, 3 * KS), lanes] = sums[: 3 * KS]
        whole[0, pl.ds(3 * KS + KL, 2), lanes] = sums[3 * KS : 3 * KS + 2]
    copy = pltpu.make_async_copy(whole, out_ref, sem)
    copy.start()
    copy.wait()


VMEM = pl.BlockSpec(memory_space=pltpu.VMEM)
HBM = pl.BlockSpec(memory_space=pltpu.HBM)


def call(kernel, name, outs, operands, scratch=(), ins=VMEM, out=VMEM, micros=1.0):
    cost = pl.CostEstimate(flops=int(micros * 4e6), bytes_accessed=int(micros * 1e6), transcendentals=0)
    return pl.pallas_call(
        kernel,
        name=name,
        out_shape=[jax.ShapeDtypeStruct(shape, dtype) for shape, dtype in outs],
        in_specs=[ins] * len(operands),
        out_specs=[out] * len(outs),
        scratch_shapes=[s if not isinstance(s, tuple) else pltpu.VMEM(*s) for s in scratch],
        cost_estimate=cost,
        compiler_params=pltpu.CompilerParams(vmem_limit_bytes=40 * 1024 * 1024),
    )(*operands)


def block(rows):
    return ((rows, SHARDS, LANES), f32)


def on_device(inputs, out_grad, short_filters, long_filters, skip_gain, norm_gain):
    chan = lax.axis_size("chan")
    width = chan * inputs.shape[2]
    params = ((PARAMS, LANES), f32)
    sums = ((2 * chan, 4, LANES), f32)
    wide = ((SHARDS * ROWS, LANES), f32)
    rows, longer, thrice, taps = block(ROWS), block(ROWS + 8), block(192), block(PARAMS)

    (packed,) = call(
        pack_kernel, "pack", [((SHARDS, 2 * ROWS, LANES), bf16)], (inputs, out_grad),
        [pltpu.SemaphoreType.DMA((2 * SHARDS,))], HBM, HBM,
    )
    arrived = lax.all_to_all(packed, "seq", 0, 0)
    own, send = call(halves_kernel, "halves", [params] * 2, (short_filters, long_filters, skip_gain, norm_gain))
    other = lax.ppermute(send, "section", [(0, 1), (1, 0)])
    taps0, taps1 = call(spread_kernel, "spread", [taps] * 2, (own, other))
    x0, part = call(open_kernel, "open", [rows, sums], (arrived,), [wide])

    def over_channels(part):
        return lax.all_to_all(part, ("section", "chan"), 0, 0)

    all_part = over_channels(part)
    (g,) = call(cotangent_kernel, "cotangent", [rows], (arrived,), [wide])
    x1, q0, k0, v0, f0, mixed0, normed0, scale0, part = call(
        functools.partial(first_kernel, width), "first", [rows] * 5 + [thrice, longer, rows, sums], (x0, all_part, taps0),
        micros=3.0,
    )
    d1, scale1, normed1, mixed1, after1, sq, sk, sv, part = call(
        functools.partial(second_kernel, width), "second", [rows, rows, longer, thrice, thrice] + [longer] * 3 + [sums],
        (x1, g, over_channels(part), taps1), [rows] * 4, micros=6.0,
    )
    all_part = over_channels(part)
    grads1, base, slope, kx, vx = call(
        functools.partial(aside_kernel, width), "aside", [((MESSAGE, LANES), f32), rows, rows, longer, longer],
        (x1, g, d1, scale1, normed1, mixed1, after1, sq, sk, sv, taps1, k0, v0), micros=2.0,
    )
    (message,) = call(
        third_kernel, "third", [((2 * SHARDS, MESSAGE, LANES), bf16)],
        (base, slope, all_part, taps0, x0, scale0, normed0, mixed0, q0, f0, kx, vx, grads1),
        [block(200)] + [longer] * 3 + [((MESSAGE, LANES), f32)], micros=3.0,
    )
    gathered = lax.all_to_all(message, ("section", "seq"), 0, 0)
    result = ((1, 3 * KS + KL + 2, 2 * LANES), f32)
    (grads,) = call(close_kernel, "close", [result], (gathered,), [result, pltpu.SemaphoreType.DMA], out=HBM)
    return grads


def solution(mesh):
    placed = (
        P(None, "seq", "chan"),
        P(None, "seq", "chan"),
        P("section", None, None, "chan"),
        P("section", None, "chan"),
        P("section", "chan"),
        P("section", "chan"),
    )
    return jax.shard_map(
        on_device, mesh=mesh, in_specs=placed, out_specs=P("section", None, "chan"), check_vma=False
    )
```

```python
import functools

import jax
import jax.numpy as jnp
from jax import lax
from jax.experimental import pallas as pl
from jax.experimental.pallas import tpu as pltpu
from jax.sharding import PartitionSpec as P

EPSILON = 1e-06
SHARDS = 8
ROWS = 64
LANES = 128
KS = 7
KL = 128
PARAMS = 152
SHORT_AT, SKIP_AT, GAIN_AT = 128, 149, 150
QUARTER = ROWS // 4
SHORT_ROWS = 24
MESSAGE = SHORT_ROWS + 32
f32 = jnp.float32
bf16 = jnp.bfloat16


def rounded(a):
    return a.astype(bf16).astype(f32)


def later(a, count):
    sub = lax.broadcasted_iota(jnp.int32, a.shape, 1)
    return jnp.where(sub >= count, pltpu.roll(a, count, 1), 0.0)


def sooner(a, count):
    sub = lax.broadcasted_iota(jnp.int32, a.shape, 1)
    return jnp.where(sub < SHARDS - count, pltpu.roll(a, SHARDS - count, 1), 0.0)


def eye():
    shape = (LANES, LANES)
    return lax.broadcasted_iota(jnp.int32, shape, 0) == lax.broadcasted_iota(jnp.int32, shape, 1)


def send_sums(out_ref, chunk_of):
    diagonal = eye()
    rows = []
    for b in range(4):
        column = jnp.sum(chunk_of(b), axis=1, keepdims=True)
        rows.append(jnp.sum(jnp.where(diagonal, column, 0.0), axis=0, keepdims=True))
    whole = jnp.concatenate(rows, axis=0)
    out_ref[...] = jnp.broadcast_to(whole[None], out_ref.shape)


def column_of(row, diagonal):
    column = jnp.sum(jnp.where(diagonal, row, 0.0), axis=1, keepdims=True)
    return jnp.broadcast_to(column, (LANES, LANES)).reshape(16, SHARDS, LANES)


def scale_and_norm(width, x_ref, sums_ref, taps, scale_ref, normed):
    total = jnp.sum(sums_ref[...], axis=0)
    scale_rows = lax.rsqrt(total * (1.0 / width) + EPSILON)
    diagonal = eye()
    gain = taps[GAIN_AT]
    for b in range(4):
        at = pl.ds(16 * b, 16)
        scale = column_of(scale_rows[b : b + 1], diagonal)
        scale_ref[at] = scale
        normed[pl.ds(8 + 16 * b, 16)] = rounded(x_ref[at] * scale * gain[None])
    normed[pl.ds(0, 8)] = later(normed[pl.ds(64, 8)], 1)


def forward(taps, normed, mixed, q_ref, k_ref, v_ref, f_ref):
    @pl.loop(0, ROWS // 8)
    def _(b):
        near = normed[pl.ds(b * 8, 16)]
        streams = []
        for i in range(3):
            total = None
            for j in range(KS):
                term = taps[SHORT_AT + KS * i + j][None] * near[8 - j : 16 - j]
                total = term if total is None else total + term
            streams.append(total)
        at = pl.ds(b * 8, 8)
        q_ref[at] = streams[0]
        k_ref[at] = streams[1]
        v_ref[at] = streams[2]
        z = rounded(streams[1] * streams[2])
        mixed[pl.ds(128 + b * 8, 8)] = z
        mixed[pl.ds(64 + b * 8, 8)] = later(z, 1)
        mixed[pl.ds(b * 8, 8)] = later(z, 2)

    skip = taps[SKIP_AT]

    @pl.loop(0, ROWS // 16)
    def _(b):
        def step(g, total):
            z = mixed[pl.ds(113 + 16 * b - 16 * g, 31)]
            w = taps[pl.ds(16 * g, 16)]
            for a in range(16):
                total = total + w[a][None] * z[15 - a : 31 - a]
            return total

        own = mixed[pl.ds(128 + 16 * b, 16)]
        f_ref[pl.ds(16 * b, 16)] = lax.fori_loop(0, KL // 16, step, skip[None] * own)


def extend_after(ref, whole):
    last = ref.shape[0] // 8 - 8
    if whole:

        @pl.loop(0, last)
        def _(b):
            a = ref[pl.ds((b % 8) * 8, 8)]
            shards = b // 8 + 1
            moved = jnp.where(shards == 1, sooner(a, 1), jnp.where(shards == 2, sooner(a, 2), sooner(a, 3)))
            ref[pl.ds(64 + b * 8, 8)] = moved
    else:
        ref[pl.ds(64, 8)] = sooner(ref[pl.ds(0, 8)], 1)


def mixed_cotangent(taps, after, start, count):
    skip = taps[SKIP_AT]

    def step(g, total):
        z = after[pl.ds(start + 16 * g, count + 15)]
        w = taps[pl.ds(16 * g, 16)]
        for a in range(16):
            total = total + w[a][None] * z[a : a + count]
        return total

    return lax.fori_loop(0, KL // 16, step, skip[None] * after[pl.ds(start, count)])


def normed_cotangent(taps, streams, start):
    total = None
    for i in range(3):
        near = streams[i][pl.ds(start, 16)]
        for j in range(KS):
            term = taps[SHORT_AT + KS * i + j][None] * near[j : j + 8]
            total = term if total is None else total + term
    return total


def over_shards(a):
    return jnp.sum(a, axis=1)


def sums_of_rows(out_ref, streams, start, near, product, gain_term):
    rows = []
    for i in range(3):
        stream = streams[i][pl.ds(start, QUARTER)]
        for j in range(KS):
            rows.append(jnp.sum(stream * near[8 - j : 8 - j + QUARTER], axis=0))
    rows.append(jnp.sum(product, axis=0))
    rows.append(gain_term)
    rows.append(jnp.zeros((SHARDS, LANES), f32))
    out_ref[pl.ds(0, SHORT_ROWS), :] = over_shards(jnp.stack(rows, axis=0))


def long_sums(out_ref, at, q, after, mixed):
    for half in range(2):
        first = q * 32 + half * 16

        def step(b, total):
            d = after[pl.ds(b * 16, 16)]
            z = mixed[pl.ds(113 + b * 16 - first, 31)]
            new = []
            for a in range(16):
                new.append(total[a] + jnp.sum(d * z[15 - a : 31 - a], axis=0))
            return jnp.stack(new, axis=0)

        sums = lax.fori_loop(0, ROWS // 16, step, jnp.zeros((16, SHARDS, LANES), f32))
        out_ref[pl.ds(at + half * 16, 16), :] = over_shards(sums)


def flat(a):
    return a.reshape(ROWS * SHARDS, LANES).astype(bf16)


def rows_of(ref, b):
    at = pl.ds(pl.multiple_of(b * 64, 64), 64)
    return ref[at, :].astype(f32).reshape(8, SHARDS, LANES)


def extend_before(own_ref, mixed):
    @pl.loop(0, ROWS // 8)
    def _(b):
        z = rows_of(own_ref, b)
        mixed[pl.ds(128 + b * 8, 8)] = z
        mixed[pl.ds(64 + b * 8, 8)] = later(z, 1)
        mixed[pl.ds(b * 8, 8)] = later(z, 2)


def pack_kernel(x_ref, g_ref, out_ref, held, sems):
    mine = pl.ds(pl.multiple_of(lax.axis_index("section") * LANES, LANES), LANES)
    copies = [pltpu.make_async_copy(ref, held.at[part], sems.at[part]) for part, ref in enumerate((x_ref, g_ref))]
    for copy in copies:
        copy.start()
    for part, copy in enumerate(copies):
        copy.wait()
        for z in range(SHARDS):
            out_ref[z, pl.ds(part * ROWS, ROWS), :] = held[part, z % 2, :, mine]


def halves_kernel(short_ref, long_ref, skip_ref, gain_ref, own_ref, send_ref):
    section = lax.axis_index("section")
    mine = pl.ds(pl.multiple_of(section * LANES, LANES), LANES)
    other = pl.ds(pl.multiple_of((1 - section) * LANES, LANES), LANES)
    for ref, half in ((own_ref, mine), (send_ref, other)):
        ref[pl.ds(0, KL), :] = long_ref[0, :, half]
        for i in range(3):
            ref[pl.ds(SHORT_AT + KS * i, KS), :] = short_ref[0, i, :, half]
        ref[pl.ds(SKIP_AT, 1), :] = skip_ref[:, half]
        ref[pl.ds(GAIN_AT, 1), :] = gain_ref[:, half]
        ref[pl.ds(PARAMS - 1, 1), :] = jnp.zeros((1, LANES), f32)


def spread(own_ref, other_ref, layer, taps):
    mine = lax.axis_index("section") == layer

    @pl.loop(0, PARAMS // 8)
    def _(g):
        at = pl.ds(pl.multiple_of(g * 8, 8), 8)
        rows = jnp.where(mine, own_ref[at, :], other_ref[at, :])
        for k in range(8):
            taps[g * 8 + k] = jnp.broadcast_to(rows[k : k + 1], (8, LANES))


def spread_kernel(own_ref, other_ref, taps0, taps1):
    spread(own_ref, other_ref, 0, taps0)
    spread(own_ref, other_ref, 1, taps1)


def open_kernel(in_ref, x_ref, g_ref, out_ref, wide):
    unpack(in_ref, 0, wide, x_ref)

    def chunk(b):
        x = x_ref[pl.ds(16 * b, 16)].reshape(LANES, LANES)
        return x * x

    send_sums(out_ref, chunk)
    unpack(in_ref, 1, wide, g_ref)


def unpack(in_ref, part, wide, ref):
    for z in range(SHARDS):
        wide[pl.ds(z * ROWS, ROWS), :] = in_ref[z, pl.ds(part * ROWS, ROWS), :].astype(f32)
    for v in range(ROWS):
        ref[v] = wide[pl.ds(v, SHARDS, stride=ROWS), :]


def first_kernel(
    width, x_ref, sums_ref, taps,
    x1_ref, q_ref, f_ref, mixed_ref, normed_part, k_part, v_part, scaled_part, out_ref,
    mixed, normed, scale_ref, k_ref, v_ref
):
    scale_and_norm(width, x_ref, sums_ref, taps, scale_ref, normed)
    forward(taps, normed, mixed, q_ref, k_ref, v_ref, f_ref)

    def chunk(b):
        at = pl.ds(16 * b, 16)
        x1 = rounded(x_ref[at] + q_ref[at] * f_ref[at])
        x1_ref[at] = x1
        return (x1 * x1).reshape(LANES, LANES)

    send_sums(out_ref, chunk)
    mixed_ref[...] = flat(mixed[pl.ds(128, ROWS)])
    start = (lax.axis_index("seq") // 2) * QUARTER
    for ref, part in ((k_ref, k_part), (v_ref, v_part)):
        extend_after(ref, False)
        part[...] = ref[pl.ds(start, QUARTER + 8)]
    normed_part[...] = normed[pl.ds(start, QUARTER + 8)]
    at = pl.ds(start, QUARTER)
    scaled_part[...] = x_ref[at] * scale_ref[at]


def second_kernel(
    width, x_ref, g_ref, sums_ref, taps,
    base_ref, slope_ref, after_ref, mixed_ref, grads_ref, out_ref,
    normed, mixed, after, sq, sk, sv, q_ref, k_ref, v_ref, f_ref, scale_ref, d_ref
):
    scale_and_norm(width, x_ref, sums_ref, taps, scale_ref, normed)
    forward(taps, normed, mixed, q_ref, k_ref, v_ref, f_ref)

    @pl.loop(0, ROWS // 8)
    def _(b):
        at = pl.ds(b * 8, 8)
        e = g_ref[at]
        sq[at] = rounded(e * f_ref[at])
        d_filtered = rounded(e * q_ref[at])
        after[at] = d_filtered

    extend_after(after, True)

    @pl.loop(0, ROWS // 16)
    def _(b):
        at = pl.ds(b * 16, 16)
        d_mixed = mixed_cotangent(taps, after, b * 16, 16)
        sk[at] = rounded(d_mixed * v_ref[at])
        sv[at] = rounded(d_mixed * k_ref[at])

    for ref in (sq, sk, sv):
        extend_after(ref, False)

    gain = taps[GAIN_AT][None]

    @pl.loop(0, ROWS // 8)
    def _(b):
        at = pl.ds(b * 8, 8)
        d_normed = normed_cotangent(taps, (sq, sk, sv), b * 8)
        scale = scale_ref[at]
        x = x_ref[at]
        d_ref[at] = gain * d_normed * x
        base_ref[at] = g_ref[at] + scale * gain * d_normed
        slope_ref[at] = x * (scale * scale * scale) * (1.0 / width)
        k_ref[at] = d_normed * x * scale

    def chunk(b):
        return d_ref[pl.ds(16 * b, 16)].reshape(LANES, LANES)

    send_sums(out_ref, chunk)
    mixed_ref[...] = flat(mixed[pl.ds(128, ROWS)])
    after_ref[...] = flat(after[pl.ds(0, ROWS)])
    start = (lax.axis_index("seq") // 2) * QUARTER
    at = pl.ds(start, QUARTER)
    sums_of_rows(
        grads_ref, (sq, sk, sv), start, normed[pl.ds(start, QUARTER + 8)],
        after[at] * mixed[pl.ds(128 + start, QUARTER)], jnp.sum(k_ref[at], axis=0),
    )


def aside_kernel(after_ref, mixed_ref, grads_ref, mixed, after):
    extend_before(mixed_ref, mixed)

    @pl.loop(0, ROWS // 8)
    def _(b):
        after[pl.ds(b * 8, 8)] = rows_of(after_ref, b)

    long_sums(grads_ref, 0, lax.axis_index("seq") // 2, after, mixed)


def third_kernel(
    base_ref, slope_ref, sums_ref, taps, scaled_part, normed_part, mixed_ref, q_ref, f_ref, k_part, v_part,
    short1_ref, long1_ref, out_ref, mixed, after, sq, sk, sv, grads
):
    q = lax.axis_index("seq") // 2
    total = jnp.sum(sums_ref[...], axis=0)
    diagonal = eye()
    for b in range(4):
        at = pl.ds(16 * b, 16)
        e = rounded(base_ref[at] - slope_ref[at] * column_of(total[b : b + 1], diagonal))
        sq[at] = rounded(e * f_ref[at])
        after[at] = rounded(e * q_ref[at])
    extend_after(after, True)
    extend_after(sq, False)
    extend_before(mixed_ref, mixed)
    start = q * QUARTER

    for part in range(2):
        at = pl.ds(start + 12 * part, 12)
        here = pl.ds(12 * part, 12)
        d_mixed = mixed_cotangent(taps, after, start + 12 * part, 12)
        sk[at] = rounded(d_mixed * v_part[here])
        sv[at] = rounded(d_mixed * k_part[here])

    gain_term = jnp.zeros((SHARDS, LANES), f32)
    for b in range(2):
        d_normed = normed_cotangent(taps, (sq, sk, sv), start + 8 * b)
        gain_term = gain_term + jnp.sum(d_normed * scaled_part[pl.ds(8 * b, 8)], axis=0)
    product = after[pl.ds(start, QUARTER)] * mixed[pl.ds(128 + start, QUARTER)]
    sums_of_rows(grads, (sq, sk, sv), start, normed_part[...], product, gain_term)
    long_sums(grads, SHORT_ROWS, q, after, mixed)
    message0 = grads[...].astype(bf16)
    message1 = jnp.concatenate([short1_ref[...], long1_ref[...]], axis=0).astype(bf16)
    for z in range(SHARDS):
        out_ref[z] = message0
        out_ref[SHARDS + z] = message1


def close_kernel(in_ref, out_ref, whole, sem):
    for half in range(2):
        lanes = pl.ds(half * LANES, LANES)
        sums = None
        for q in range(4):
            pair = in_ref[half * SHARDS + 2 * q].astype(f32) + in_ref[half * SHARDS + 2 * q + 1].astype(f32)
            whole[0, pl.ds(3 * KS + 32 * q, 32), lanes] = pair[SHORT_ROWS:]
            sums = pair[:SHORT_ROWS] if sums is None else sums + pair[:SHORT_ROWS]
        whole[0, pl.ds(0, 3 * KS), lanes] = sums[: 3 * KS]
        whole[0, pl.ds(3 * KS + KL, 2), lanes] = sums[3 * KS : 3 * KS + 2]
    copy = pltpu.make_async_copy(whole, out_ref, sem)
    copy.start()
    copy.wait()


VMEM = pl.BlockSpec(memory_space=pltpu.VMEM)
HBM = pl.BlockSpec(memory_space=pltpu.HBM)


def call(kernel, name, outs, operands, scratch=(), ins=VMEM, out=VMEM, flops=0):
    cost = pl.CostEstimate(flops=flops, bytes_accessed=0, transcendentals=0) if flops else None
    return pl.pallas_call(
        kernel,
        name=name,
        out_shape=[jax.ShapeDtypeStruct(shape, dtype) for shape, dtype in outs],
        in_specs=[ins] * len(operands),
        out_specs=[out] * len(outs),
        scratch_shapes=[s if not isinstance(s, tuple) else pltpu.VMEM(*s) for s in scratch],
        cost_estimate=cost,
        compiler_params=pltpu.CompilerParams(vmem_limit_bytes=20 * 1024 * 1024),
    )(*operands)


def block(rows):
    return ((rows, SHARDS, LANES), f32)


def on_device(inputs, out_grad, short_filters, long_filters, skip_gain, norm_gain):
    chan = lax.axis_size("chan")
    width = chan * inputs.shape[2]
    params = ((PARAMS, LANES), f32)
    sums = ((2 * chan, 4, LANES), f32)
    wide = ((SHARDS * ROWS, LANES), f32)
    rows, longer, thrice, taps, part_rows = block(ROWS), block(ROWS + 8), block(192), block(PARAMS), block(QUARTER + 8)
    kept = ((SHARDS * ROWS, LANES), bf16)
    shorts, longs = ((SHORT_ROWS, LANES), f32), ((32, LANES), f32)

    (packed,) = call(
        pack_kernel, "pack", [((SHARDS, 2 * ROWS, LANES), bf16)],
        tuple(pltpu.with_memory_space_constraint(a, pltpu.HBM) for a in (inputs, out_grad)),
        [((2, 2, ROWS, 2 * LANES), bf16), pltpu.SemaphoreType.DMA((2,))], HBM,
    )
    arrived = lax.all_to_all(packed, "seq", 0, 0)
    own, send = call(halves_kernel, "halves", [params] * 2, (short_filters, long_filters, skip_gain, norm_gain))
    other = lax.ppermute(send, "section", [(0, 1), (1, 0)])
    taps0, taps1 = call(spread_kernel, "spread", [taps] * 2, (own, other))
    x0, g, part = call(open_kernel, "open", [rows, rows, sums], (arrived,), [wide])

    def over_channels(part):
        return lax.all_to_all(part, ("section", "chan"), 0, 0)

    x1, q0, f0, mixed0, normed0, k0, v0, scaled0, part = call(
        functools.partial(first_kernel, width), "first",
        [rows] * 3 + [kept] + [part_rows] * 3 + [block(QUARTER), sums], (x0, over_channels(part), taps0),
        [thrice, longer, rows, longer, longer],
    )
    base, slope, after1, mixed1, short1, part = call(
        functools.partial(second_kernel, width), "second", [rows] * 2 + [kept] * 2 + [shorts, sums],
        (x1, g, over_channels(part), taps1), [longer, thrice, thrice] + [longer] * 3 + [rows] * 6,
    )
    all_part = over_channels(part)
    (long1,) = call(aside_kernel, "aside", [longs], (after1, mixed1), [thrice, rows], flops=2000000)
    (message,) = call(
        third_kernel, "third", [((2 * SHARDS, MESSAGE, LANES), bf16)],
        (base, slope, all_part, taps0, scaled0, normed0, mixed0, q0, f0, k0, v0, short1, long1),
        [thrice, block(200)] + [longer] * 3 + [((MESSAGE, LANES), f32)],
    )
    gathered = lax.all_to_all(message, ("section", "seq"), 0, 0)
    result = ((1, 3 * KS + KL + 2, 2 * LANES), f32)
    (grads,) = call(close_kernel, "close", [result], (gathered,), [result, pltpu.SemaphoreType.DMA], out=HBM)
    return grads


def solution(mesh):
    placed = (
        P(None, "seq", "chan"),
        P(None, "seq", "chan"),
        P("section", None, None, "chan"),
        P("section", None, "chan"),
        P("section", "chan"),
        P("section", "chan"),
    )
    return jax.shard_map(
        on_device, mesh=mesh, in_specs=placed, out_specs=P("section", None, "chan"), check_vma=False
    )
```

```python
import functools

import jax
import jax.numpy as jnp
from jax import lax
from jax.experimental import pallas as pl
from jax.experimental.pallas import tpu as pltpu
from jax.sharding import PartitionSpec as P

EPSILON = 1e-06
SHARDS = 8
ROWS = 64
LANES = 128
KS = 7
KL = 128
PARAMS = 152
PARTS = 9
SHORT_AT, SKIP_AT, GAIN_AT, TAPS = 288, 309, 310, 312
QUARTER = ROWS // 4
SHORT_ROWS = 24
MESSAGE = SHORT_ROWS + 32
f32 = jnp.float32
bf16 = jnp.bfloat16


def rounded(a):
    return a.astype(bf16).astype(f32)


def later(a, count):
    sub = lax.broadcasted_iota(jnp.int32, a.shape, 1)
    return jnp.where(sub >= count, pltpu.roll(a, count, 1), 0.0)


def sooner(a, count):
    sub = lax.broadcasted_iota(jnp.int32, a.shape, 1)
    return jnp.where(sub < SHARDS - count, pltpu.roll(a, SHARDS - count, 1), 0.0)


def eye():
    shape = (LANES, LANES)
    return lax.broadcasted_iota(jnp.int32, shape, 0) == lax.broadcasted_iota(jnp.int32, shape, 1)


def send_sums(out_ref, chunk_of):
    diagonal = eye()
    rows = []
    for b in range(4):
        column = jnp.sum(chunk_of(b), axis=1, keepdims=True)
        rows.append(jnp.sum(jnp.where(diagonal, column, 0.0), axis=0, keepdims=True))
    whole = jnp.concatenate(rows, axis=0)
    out_ref[...] = jnp.broadcast_to(whole[None], out_ref.shape)


def column_of(row, diagonal):
    column = jnp.sum(jnp.where(diagonal, row, 0.0), axis=1, keepdims=True)
    return jnp.broadcast_to(column, (LANES, LANES)).reshape(16, SHARDS, LANES)


def sixteen_of(ref, b):
    if len(ref.shape) == 3:
        return ref[pl.ds(16 * b, 16)]
    at = pl.ds(pl.multiple_of(b * LANES, LANES), LANES)
    return ref[at, :].astype(f32).reshape(16, SHARDS, LANES)


def scale_and_norm(width, x_ref, sums_ref, taps, scale_ref, normed):
    total = jnp.sum(sums_ref[...], axis=0)
    scale_rows = lax.rsqrt(total * (1.0 / width) + EPSILON)
    diagonal = eye()
    gain = taps[GAIN_AT]
    for b in range(4):
        scale = column_of(scale_rows[b : b + 1], diagonal)
        scale_ref[pl.ds(16 * b, 16)] = scale
        normed[pl.ds(8 + 16 * b, 16)] = rounded(sixteen_of(x_ref, b) * scale * gain[None])
    normed[pl.ds(0, 8)] = later(normed[pl.ds(64, 8)], 1)
    return scale_rows


def forward(taps, normed, mixed, signals, results, q_ref, k_ref, v_ref, f_ref):
    @pl.loop(0, ROWS // 8)
    def _(b):
        near = normed[pl.ds(b * 8, 16)]
        streams = []
        for i in range(3):
            total = None
            for j in range(KS):
                term = taps[SHORT_AT + KS * i + j][None] * near[8 - j : 16 - j]
                total = term if total is None else total + term
            streams.append(total)
        at = pl.ds(b * 8, 8)
        q_ref[at] = streams[0]
        k_ref[at] = streams[1]
        v_ref[at] = streams[2]
        z = rounded(streams[1] * streams[2])
        mixed[pl.ds(128 + b * 8, 8)] = z
        mixed[pl.ds(64 + b * 8, 8)] = later(z, 1)
        mixed[pl.ds(b * 8, 8)] = later(z, 2)

    split(mixed, 1, signals, REVERSED, 6)
    convolve(taps, signals, results, True, 16)
    skip = taps[SKIP_AT][None]
    for half in range(2):
        at = pl.ds(32 * half, 32)
        f_ref[at] = skip * mixed[pl.ds(128 + 32 * half, 32)] + joined(results, REVERSED, 8 * half, 8)


def split(ref, start, signals, order, blocks):
    @pl.loop(0, blocks)
    def _(g):
        near = ref[pl.ds(start + 32 * g, 32)].reshape(8, 4, SHARDS, LANES)
        far = ref[pl.ds(start + 4 + 32 * g, 32)].reshape(8, 4, SHARDS, LANES)
        s = [near[:, 0], near[:, 1], near[:, 2], near[:, 3], far[:, 0], far[:, 1], far[:, 2]]
        one = (s[1], s[3], s[5])
        two = (s[0] - s[1], s[2] - s[3], s[4] - s[5])
        three = (s[2] - s[1], s[4] - s[3], s[6] - s[5])
        for t, (before, middle, after) in enumerate((one, two, three)):
            for p, part in enumerate((middle, before - middle, after - middle)):
                signals[order[3 * t + p], pl.ds(8 * g, 8)] = part


STRAIGHT = (0, 1, 2, 3, 4, 5, 6, 7, 8)
REVERSED = (0, 2, 1, 6, 8, 7, 3, 5, 4)


def convolve(taps, signals, results, backwards, count):
    @pl.loop(0, PARTS)
    def _(u):
        total = jnp.zeros((count, SHARDS, LANES), f32)
        for g in range(2):
            z = signals[u, pl.ds(16 * g, count + 15)]
            w = taps[pl.ds(32 * u + 16 * (1 - g if backwards else g), 16)]
            for a in range(16):
                total = total + w[15 - a if backwards else a][None] * z[a : a + count]
        results[u, pl.ds(0, count)] = total


def joined(results, order, start, count):
    even, odd = [], []
    for t in range(3):
        middle, first, last = (results[order[3 * t + p], pl.ds(start, count)] for p in range(3))
        even.append(middle + first)
        odd.append(middle + last)
    rows = [even[0] + even[1], even[0] + even[2], odd[0] + odd[1], odd[0] + odd[2]]
    return jnp.stack(rows, axis=1).reshape(4 * count, SHARDS, LANES)


def extend_after(ref, blocks):
    if blocks > 1:

        @pl.loop(0, blocks)
        def _(b):
            a = ref[pl.ds((b % 8) * 8, 8)]
            shards = b // 8 + 1
            moved = jnp.where(shards == 1, sooner(a, 1), jnp.where(shards == 2, sooner(a, 2), sooner(a, 3)))
            ref[pl.ds(64 + b * 8, 8)] = moved
    else:
        ref[pl.ds(64, 8)] = sooner(ref[pl.ds(0, 8)], 1)


def normed_cotangent(taps, streams, start):
    total = None
    for i in range(3):
        near = streams[i][pl.ds(start, 16)]
        for j in range(KS):
            term = taps[SHORT_AT + KS * i + j][None] * near[j : j + 8]
            total = term if total is None else total + term
    return total


def over_shards(a):
    return jnp.sum(a, axis=1)


def sums_of_rows(out_ref, streams, start, near, product, gain_term):
    rows = []
    for i in range(3):
        stream = streams[i][pl.ds(start, QUARTER)]
        for j in range(KS):
            rows.append(jnp.sum(stream * near[8 - j : 8 - j + QUARTER], axis=0))
    rows.append(jnp.sum(product, axis=0))
    rows.append(gain_term)
    rows.append(jnp.zeros((SHARDS, LANES), f32))
    out_ref[pl.ds(0, SHORT_ROWS), :] = over_shards(jnp.stack(rows, axis=0))


def long_sums(out_ref, at, q, after, mixed):
    for half in range(2):
        first = q * 32 + half * 16

        def step(b, total):
            d = after[pl.ds(b * 16, 16)]
            z = mixed[pl.ds(113 + b * 16 - first, 31)]
            new = []
            for a in range(16):
                new.append(total[a] + jnp.sum(d * z[15 - a : 31 - a], axis=0))
            return jnp.stack(new, axis=0)

        sums = lax.fori_loop(0, ROWS // 16, step, jnp.zeros((16, SHARDS, LANES), f32))
        out_ref[pl.ds(at + half * 16, 16), :] = over_shards(sums)


def flat(a):
    return a.reshape(ROWS * SHARDS, LANES).astype(bf16)


def rows_of(ref, b):
    at = pl.ds(pl.multiple_of(b * 64, 64), 64)
    return ref[at, :].astype(f32).reshape(8, SHARDS, LANES)


def extend_before(own_ref, mixed):
    @pl.loop(0, ROWS // 8)
    def _(b):
        z = rows_of(own_ref, b)
        mixed[pl.ds(128 + b * 8, 8)] = z
        mixed[pl.ds(64 + b * 8, 8)] = later(z, 1)
        mixed[pl.ds(b * 8, 8)] = later(z, 2)


def pack_kernel(x_ref, g_ref, out_ref, held, sems):
    mine = pl.ds(pl.multiple_of(lax.axis_index("section") * LANES, LANES), LANES)
    copies = [pltpu.make_async_copy(ref, held.at[part], sems.at[part]) for part, ref in enumerate((x_ref, g_ref))]
    for copy in copies:
        copy.start()
    for part, copy in enumerate(copies):
        copy.wait()
        for z in range(SHARDS):
            out_ref[z, pl.ds(part * ROWS, ROWS), :] = held[part, z % 2, :, mine]


def halves_kernel(short_ref, long_ref, skip_ref, gain_ref, own_ref, send_ref):
    section = lax.axis_index("section")
    mine = pl.ds(pl.multiple_of(section * LANES, LANES), LANES)
    other = pl.ds(pl.multiple_of((1 - section) * LANES, LANES), LANES)
    for ref, half in ((own_ref, mine), (send_ref, other)):
        ref[pl.ds(0, KL), :] = long_ref[0, :, half]
        for i in range(3):
            ref[pl.ds(KL + KS * i, KS), :] = short_ref[0, i, :, half]
        ref[pl.ds(KL + 3 * KS, 1), :] = skip_ref[:, half]
        ref[pl.ds(KL + 3 * KS + 1, 1), :] = gain_ref[:, half]
        ref[pl.ds(PARAMS - 1, 1), :] = jnp.zeros((1, LANES), f32)


def spread(own_ref, other_ref, layer, taps):
    mine = lax.axis_index("section") == layer

    def rows_at(g):
        at = pl.ds(pl.multiple_of(g * 8, 8), 8)
        rows = jnp.where(mine, own_ref[at, :], other_ref[at, :])
        return [jnp.broadcast_to(rows[k : k + 1], (8, LANES)) for k in range(8)]

    @pl.loop(0, KL // 8)
    def _(g):
        rows = rows_at(g)
        for half in range(2):
            a, b, c, d = rows[4 * half : 4 * half + 4]
            parts = (a + b + (c + d), a + b, c + d, a + c, a, c, b + d, b, d)
            for u, part in enumerate(parts):
                taps[32 * u + 2 * g + half] = part

    for g in range(3):
        for k, row in enumerate(rows_at(KL // 8 + g)):
            taps[SHORT_AT + 8 * g + k] = row


def spread_kernel(own_ref, other_ref, taps0, token_ref):
    spread(own_ref, other_ref, 0, taps0)
    token_ref[...] = jnp.zeros_like(token_ref)


def open_kernel(in_ref, token_ref, x_ref, g_ref, out_ref, wide):
    unpack(in_ref, 0, wide, x_ref)

    def chunk(b):
        x = x_ref[pl.ds(16 * b, 16)].reshape(LANES, LANES)
        return x * x

    send_sums(out_ref, chunk)
    unpack(in_ref, 1, wide, g_ref)


def unpack(in_ref, part, wide, ref):
    for z in range(SHARDS):
        wide[pl.ds(z * ROWS, ROWS), :] = in_ref[z, pl.ds(part * ROWS, ROWS), :].astype(f32)
    for v in range(ROWS):
        ref[v] = wide[pl.ds(v, SHARDS, stride=ROWS), :]


def first_kernel(
    width, x_ref, sums_ref, taps,
    x1_ref, q_ref, mixed_ref, normed_part, f_part, k_part, v_part, scaled_part, out_ref,
    mixed, normed, scale_ref, f_ref, k_ref, v_ref, signals, results
):
    scale_and_norm(width, x_ref, sums_ref, taps, scale_ref, normed)
    forward(taps, normed, mixed, signals, results, q_ref, k_ref, v_ref, f_ref)

    def chunk(b):
        at = pl.ds(16 * b, 16)
        x1 = rounded(x_ref[at] + q_ref[at] * f_ref[at])
        x1 = x1.reshape(LANES, LANES)
        x1_ref[pl.ds(LANES * b, LANES), :] = x1.astype(bf16)
        return x1 * x1

    send_sums(out_ref, chunk)
    mixed_ref[...] = flat(mixed[pl.ds(128, ROWS)])
    start = (lax.axis_index("seq") // 2) * QUARTER
    for ref, part in ((f_ref, f_part), (k_ref, k_part), (v_ref, v_part)):
        extend_after(ref, 1)
        part[...] = ref[pl.ds(start, QUARTER + 8)]
    normed_part[...] = normed[pl.ds(start, QUARTER + 8)]
    at = pl.ds(start, QUARTER)
    scaled_part[...] = x_ref[at] * scale_ref[at]


def second_kernel(
    width, x_ref, g_ref, sums_ref, own_ref, other_ref,
    base_ref, cubes_ref, after_ref, mixed_ref, grads_ref, out_ref,
    normed, mixed, after, sq, sk, sv, q_ref, k_ref, v_ref, f_ref, scale_ref, d_ref, signals, results, taps, parts, sem
):
    spread(own_ref, other_ref, 1, taps)
    scale_rows = scale_and_norm(width, x_ref, sums_ref, taps, scale_ref, normed)
    cubes_ref[...] = scale_rows * scale_rows * scale_rows * (1.0 / width)
    forward(taps, normed, mixed, signals, results, q_ref, k_ref, v_ref, f_ref)

    @pl.loop(0, ROWS // 8)
    def _(b):
        at = pl.ds(b * 8, 8)
        e = g_ref[at]
        sq[at] = rounded(e * f_ref[at])
        d_filtered = rounded(e * q_ref[at])
        after[at] = d_filtered

    extend_after(after, 17)

    split(after, 0, signals, STRAIGHT, 6)
    convolve(taps, signals, results, False, 16)
    skip = taps[SKIP_AT][None]
    for half in range(2):
        at = pl.ds(32 * half, 32)
        d_mixed = skip * after[at] + joined(results, STRAIGHT, 8 * half, 8)
        sk[at] = rounded(d_mixed * v_ref[at])
        sv[at] = rounded(d_mixed * k_ref[at])

    for ref in (sq, sk, sv):
        extend_after(ref, 1)

    gain = taps[GAIN_AT][None]

    @pl.loop(0, ROWS // 8)
    def _(b):
        at = pl.ds(b * 8, 8)
        d_normed = normed_cotangent(taps, (sq, sk, sv), b * 8)
        scale = scale_ref[at]
        x = rows_of(x_ref, b)
        d_ref[at] = gain * d_normed * x
        base_ref[at] = g_ref[at] + scale * gain * d_normed
        k_ref[at] = d_normed * x * scale

    def chunk(b):
        return d_ref[pl.ds(16 * b, 16)].reshape(LANES, LANES)

    send_sums(parts, chunk)
    copy = pltpu.make_async_copy(parts, out_ref, sem)
    copy.start()
    mixed_ref[...] = flat(mixed[pl.ds(128, ROWS)])
    after_ref[...] = flat(after[pl.ds(0, ROWS)])
    start = (lax.axis_index("seq") // 2) * QUARTER
    at = pl.ds(start, QUARTER)
    sums_of_rows(
        grads_ref, (sq, sk, sv), start, normed[pl.ds(start, QUARTER + 8)],
        after[at] * mixed[pl.ds(128 + start, QUARTER)], jnp.sum(k_ref[at], axis=0),
    )
    copy.wait()


def aside_kernel(after_ref, mixed_ref, grads_ref, mixed, after):
    extend_before(mixed_ref, mixed)

    @pl.loop(0, ROWS // 8)
    def _(b):
        after[pl.ds(b * 8, 8)] = rows_of(after_ref, b)

    long_sums(grads_ref, 0, lax.axis_index("seq") // 2, after, mixed)


def third_kernel(
    base_ref, x1_ref, cubes_ref, sums_ref, own_ref, other_ref, scaled_part, normed_part, mixed_ref, q_ref, f_part, k_part, v_part,
    short1_ref, long1_ref, out_ref, mixed, after, errors, sq, sk, sv, grads, signals, results, taps
):
    spread(own_ref, other_ref, 0, taps)
    q = lax.axis_index("seq") // 2
    total = jnp.sum(sums_ref[...], axis=0) * cubes_ref[...]
    diagonal = eye()
    for b in range(4):
        at = pl.ds(16 * b, 16)
        e = rounded(base_ref[at] - sixteen_of(x1_ref, b) * column_of(total[b : b + 1], diagonal))
        errors[at] = e
        after[at] = rounded(e * q_ref[at])
    extend_after(after, 17)
    extend_after(errors, 1)
    extend_before(mixed_ref, mixed)
    start = q * QUARTER

    split(after, start, signals, STRAIGHT, 5)
    convolve(taps, signals, results, False, 6)
    at = pl.ds(start, QUARTER + 8)
    d_mixed = taps[SKIP_AT][None] * after[at] + joined(results, STRAIGHT, 0, 6)
    sq[at] = rounded(errors[at] * f_part[...])
    sk[at] = rounded(d_mixed * v_part[...])
    sv[at] = rounded(d_mixed * k_part[...])

    gain_term = jnp.zeros((SHARDS, LANES), f32)
    for b in range(2):
        d_normed = normed_cotangent(taps, (sq, sk, sv), start + 8 * b)
        gain_term = gain_term + jnp.sum(d_normed * scaled_part[pl.ds(8 * b, 8)], axis=0)
    product = after[pl.ds(start, QUARTER)] * mixed[pl.ds(128 + start, QUARTER)]
    sums_of_rows(grads, (sq, sk, sv), start, normed_part[...], product, gain_term)
    long_sums(grads, SHORT_ROWS, q, after, mixed)
    message0 = grads[...].astype(bf16)
    message1 = jnp.concatenate([short1_ref[...], long1_ref[...]], axis=0).astype(bf16)
    for z in range(SHARDS):
        out_ref[z] = message0
        out_ref[SHARDS + z] = message1


def close_kernel(in_ref, out_ref, whole):
    for half in range(2):
        lanes = pl.ds(half * LANES, LANES)
        sums = None
        for q in range(4):
            pair = in_ref[half * SHARDS + 2 * q].astype(f32) + in_ref[half * SHARDS + 2 * q + 1].astype(f32)
            whole[pl.ds(3 * KS + 32 * q, 32), lanes] = pair[SHORT_ROWS:]
            sums = pair[:SHORT_ROWS] if sums is None else sums + pair[:SHORT_ROWS]
        whole[pl.ds(0, 3 * KS), lanes] = sums[: 3 * KS]
        whole[pl.ds(3 * KS + KL, 2), lanes] = sums[3 * KS : 3 * KS + 2]
    out_ref[...] = whole[...].reshape(out_ref.shape)


VMEM = pl.BlockSpec(memory_space=pltpu.VMEM)
HBM = pl.BlockSpec(memory_space=pltpu.HBM)


def call(kernel, name, outs, operands, scratch=(), ins=VMEM, in_hbm=None, flops=0):
    cost = pl.CostEstimate(flops=flops, bytes_accessed=0, transcendentals=0) if flops else None
    return pl.pallas_call(
        kernel,
        name=name,
        out_shape=[jax.ShapeDtypeStruct(shape, dtype) for shape, dtype in outs],
        in_specs=[ins] * len(operands),
        out_specs=[HBM if i == in_hbm else VMEM for i in range(len(outs))],
        scratch_shapes=[s if not isinstance(s, tuple) else pltpu.VMEM(*s) for s in scratch],
        cost_estimate=cost,
        compiler_params=pltpu.CompilerParams(vmem_limit_bytes=20 * 1024 * 1024),
    )(*operands)


def block(rows):
    return ((rows, SHARDS, LANES), f32)


def on_device(inputs, out_grad, short_filters, long_filters, skip_gain, norm_gain):
    chan = lax.axis_size("chan")
    width = chan * inputs.shape[2]
    params = ((PARAMS, LANES), f32)
    sums = ((2 * chan, 4, LANES), f32)
    wide = ((SHARDS * ROWS, LANES), f32)
    rows, longer, thrice, taps, part_rows = block(ROWS), block(ROWS + 8), block(200), block(TAPS), block(QUARTER + 8)
    splits = [((PARTS, 48, SHARDS, LANES), f32), ((PARTS, 16, SHARDS, LANES), f32)]
    kept = ((SHARDS * ROWS, LANES), bf16)
    shorts, longs = ((SHORT_ROWS, LANES), f32), ((32, LANES), f32)

    (packed,) = call(
        pack_kernel, "pack", [((SHARDS, 2 * ROWS, LANES), bf16)],
        tuple(pltpu.with_memory_space_constraint(a, pltpu.HBM) for a in (inputs, out_grad)),
        [((2, 2, ROWS, 2 * LANES), bf16), pltpu.SemaphoreType.DMA((2,))], HBM,
    )
    arrived = lax.all_to_all(packed, "seq", 0, 0)
    own, send = call(halves_kernel, "halves", [params] * 2, (short_filters, long_filters, skip_gain, norm_gain))
    other = lax.ppermute(send, "section", [(0, 1), (1, 0)])
    taps0, token = call(spread_kernel, "spread", [taps, block(1)], (own, other))
    x0, g, part = call(open_kernel, "open", [rows, rows, sums], (arrived, token), [wide])

    def over_channels(part):
        return lax.all_to_all(part, ("section", "chan"), 0, 0)

    x1, q0, mixed0, normed0, f0, k0, v0, scaled0, part = call(
        functools.partial(first_kernel, width), "first",
        [kept, rows, kept] + [part_rows] * 4 + [block(QUARTER), sums], (x0, over_channels(part), taps0),
        [thrice, longer, rows, longer, longer, longer] + splits,
    )
    base, cubes, after1, mixed1, short1, part = call(
        functools.partial(second_kernel, width), "second",
        [rows, ((4, LANES), f32), kept, kept, shorts, sums], (x1, g, over_channels(part), own, other),
        [longer, thrice, thrice] + [longer] * 3 + [rows] * 6 + splits + [taps, sums, pltpu.SemaphoreType.DMA], in_hbm=5,
    )
    all_part = over_channels(part)
    (long1,) = call(aside_kernel, "aside", [longs], (after1, mixed1), [thrice, rows], flops=2000000)
    (message,) = call(
        third_kernel, "third", [((2 * SHARDS, MESSAGE, LANES), bf16)],
        (base, x1, cubes, all_part, own, other, scaled0, normed0, mixed0, q0, f0, k0, v0, short1, long1),
        [thrice, block(216)] + [longer] * 4 + [((MESSAGE, LANES), f32)] + splits + [taps],
    )
    gathered = lax.all_to_all(message, ("section", "seq"), 0, 0)
    count = 3 * KS + KL + 2
    (grads,) = call(
        close_kernel, "close", [((count, 1, 2 * LANES), f32)], (gathered,), [((count, 2 * LANES), f32)]
    )
    return grads.transpose(1, 0, 2)


def solution(mesh):
    placed = (
        P(None, "seq", "chan"),
        P(None, "seq", "chan"),
        P("section", None, None, "chan"),
        P("section", None, "chan"),
        P("section", "chan"),
        P("section", "chan"),
    )
    return jax.shard_map(
        on_device, mesh=mesh, in_specs=placed, out_specs=P("section", None, "chan"), check_vma=False
    )
```

```python
import functools

import jax
import jax.numpy as jnp
from jax import lax
from jax.experimental import pallas as pl
from jax.experimental.pallas import tpu as pltpu
from jax.sharding import PartitionSpec as P

EPSILON = 1e-06
SHARDS = 8
ROWS = 64
LANES = 128
KS = 7
KL = 128
PARAMS = 152
UNROLLED = 3
PARTS = 9
SHORT_AT, SKIP_AT, GAIN_AT, TAPS = 288, 309, 310, 312
QUARTER = ROWS // 4
SHORT_ROWS = 24
MESSAGE = SHORT_ROWS + 32
f32 = jnp.float32
bf16 = jnp.bfloat16


def rounded(a):
    return a.astype(bf16).astype(f32)


def later(a, count):
    sub = lax.broadcasted_iota(jnp.int32, a.shape, 1)
    return jnp.where(sub >= count, pltpu.roll(a, count, 1), 0.0)


def sooner(a, count):
    sub = lax.broadcasted_iota(jnp.int32, a.shape, 1)
    return jnp.where(sub < SHARDS - count, pltpu.roll(a, SHARDS - count, 1), 0.0)


def eye():
    shape = (LANES, LANES)
    return lax.broadcasted_iota(jnp.int32, shape, 0) == lax.broadcasted_iota(jnp.int32, shape, 1)


def send_sums(out_ref, chunk_of):
    diagonal = eye()
    rows = []
    for b in range(4):
        column = jnp.sum(chunk_of(b), axis=1, keepdims=True)
        rows.append(jnp.sum(jnp.where(diagonal, column, 0.0), axis=0, keepdims=True))
    whole = jnp.concatenate(rows, axis=0)
    out_ref[...] = jnp.broadcast_to(whole[None], out_ref.shape)


def column_of(row, diagonal):
    column = jnp.sum(jnp.where(diagonal, row, 0.0), axis=1, keepdims=True)
    return jnp.broadcast_to(column, (LANES, LANES)).reshape(16, SHARDS, LANES)


def sixteen_of(ref, b):
    if len(ref.shape) == 3:
        return ref[pl.ds(16 * b, 16)]
    at = pl.ds(pl.multiple_of(b * LANES, LANES), LANES)
    return ref[at, :].astype(f32).reshape(16, SHARDS, LANES)


def scale_and_norm(width, x_ref, sums_ref, taps, scale_ref, normed):
    total = jnp.sum(sums_ref[...], axis=0)
    scale_rows = lax.rsqrt(total * (1.0 / width) + EPSILON)
    diagonal = eye()
    gain = taps[GAIN_AT]
    for b in range(4):
        scale = column_of(scale_rows[b : b + 1], diagonal)
        scale_ref[pl.ds(16 * b, 16)] = scale
        normed[pl.ds(8 + 16 * b, 16)] = rounded(sixteen_of(x_ref, b) * scale * gain[None])
    normed[pl.ds(0, 8)] = later(normed[pl.ds(64, 8)], 1)
    return scale_rows


def forward(taps, normed, mixed, signals, results, q_ref, k_ref, v_ref, f_ref):
    @pl.loop(0, ROWS // 8)
    def _(b):
        near = normed[pl.ds(b * 8, 16)]
        streams = []
        for i in range(3):
            total = None
            for j in range(KS):
                term = taps[SHORT_AT + KS * i + j][None] * near[8 - j : 16 - j]
                total = term if total is None else total + term
            streams.append(total)
        at = pl.ds(b * 8, 8)
        q_ref[at] = streams[0]
        k_ref[at] = streams[1]
        v_ref[at] = streams[2]
        z = rounded(streams[1] * streams[2])
        mixed[pl.ds(128 + b * 8, 8)] = z
        mixed[pl.ds(64 + b * 8, 8)] = later(z, 1)
        mixed[pl.ds(b * 8, 8)] = later(z, 2)

    split(mixed, 1, signals, REVERSED, 6)
    convolve(taps, signals, results, True, 16)
    skip = taps[SKIP_AT][None]
    for half in range(2):
        at = pl.ds(32 * half, 32)
        f_ref[at] = skip * mixed[pl.ds(128 + 32 * half, 32)] + joined(results, REVERSED, 8 * half, 8)


def split(ref, start, signals, order, blocks):
    @pl.loop(0, blocks)
    def _(g):
        near = ref[pl.ds(start + 32 * g, 32)].reshape(8, 4, SHARDS, LANES)
        far = ref[pl.ds(start + 4 + 32 * g, 32)].reshape(8, 4, SHARDS, LANES)
        s = [near[:, 0], near[:, 1], near[:, 2], near[:, 3], far[:, 0], far[:, 1], far[:, 2]]
        one = (s[1], s[3], s[5])
        two = (s[0] - s[1], s[2] - s[3], s[4] - s[5])
        three = (s[2] - s[1], s[4] - s[3], s[6] - s[5])
        for t, (before, middle, after) in enumerate((one, two, three)):
            for p, part in enumerate((middle, before - middle, after - middle)):
                signals[order[3 * t + p], pl.ds(8 * g, 8)] = part


STRAIGHT = (0, 1, 2, 3, 4, 5, 6, 7, 8)
REVERSED = (0, 2, 1, 6, 8, 7, 3, 5, 4)


def convolve(taps, signals, results, backwards, count):
    @pl.loop(0, PARTS // UNROLLED)
    def _(several):
        for one in range(UNROLLED):
            u = several * UNROLLED + one
            total = jnp.zeros((count, SHARDS, LANES), f32)
            for g in range(2):
                z = signals[u, pl.ds(16 * g, count + 15)]
                w = taps[pl.ds(32 * u + 16 * (1 - g if backwards else g), 16)]
                for a in range(16):
                    total = total + w[15 - a if backwards else a][None] * z[a : a + count]
            results[u, pl.ds(0, count)] = total


def joined(results, order, start, count):
    even, odd = [], []
    for t in range(3):
        middle, first, last = (results[order[3 * t + p], pl.ds(start, count)] for p in range(3))
        even.append(middle + first)
        odd.append(middle + last)
    rows = [even[0] + even[1], even[0] + even[2], odd[0] + odd[1], odd[0] + odd[2]]
    return jnp.stack(rows, axis=1).reshape(4 * count, SHARDS, LANES)


def extend_after(ref, blocks):
    if blocks == 1:
        ref[pl.ds(64, 8)] = sooner(ref[pl.ds(0, 8)], 1)
        return

    @pl.loop(0, 8)
    def _(b):
        a = ref[pl.ds(b * 8, 8)]
        ref[pl.ds(64 + b * 8, 8)] = sooner(a, 1)
        ref[pl.ds(128 + b * 8, 8)] = sooner(a, 2)

    ref[pl.ds(192, 8)] = sooner(ref[pl.ds(0, 8)], 3)


def normed_cotangent(taps, streams, start):
    total = None
    for i in range(3):
        near = streams[i][pl.ds(start, 16)]
        for j in range(KS):
            term = taps[SHORT_AT + KS * i + j][None] * near[j : j + 8]
            total = term if total is None else total + term
    return total


def over_shards(a):
    return jnp.sum(a, axis=1)


def sums_of_rows(out_ref, streams, start, near, product, gain_term):
    rows = []
    for i in range(3):
        stream = streams[i][pl.ds(start, QUARTER)]
        for j in range(KS):
            rows.append(jnp.sum(stream * near[8 - j : 8 - j + QUARTER], axis=0))
    rows.append(jnp.sum(product, axis=0))
    rows.append(gain_term)
    rows.append(jnp.zeros((SHARDS, LANES), f32))
    out_ref[pl.ds(0, SHORT_ROWS), :] = over_shards(jnp.stack(rows, axis=0))


def long_sums(out_ref, at, after, window):
    for half in range(2):
        sums = [None] * 16
        for b in range(ROWS // 16):
            d = after[pl.ds(b * 16, 16)]
            z = window[pl.ds(17 + 16 * (b - half), 31)]
            for a in range(16):
                term = jnp.sum(d * z[15 - a : 31 - a], axis=0)
                sums[a] = term if b == 0 else sums[a] + term
        out_ref[pl.ds(at + half * 16, 16), :] = over_shards(jnp.stack(sums, axis=0))


def flat(a):
    return a.reshape(ROWS * SHARDS, LANES).astype(bf16)


def rows_of(ref, b):
    at = pl.ds(pl.multiple_of(b * 64, 64), 64)
    return ref[at, :].astype(f32).reshape(8, SHARDS, LANES)


def window_before(own_ref, q, window):
    @pl.loop(0, 14)
    def _(b):
        block = 12 - 4 * q + b
        z = rows_of(own_ref, block % 8)
        back = block // 8
        window[pl.ds(8 * b, 8)] = jnp.where(back == 2, z, jnp.where(back == 1, later(z, 1), later(z, 2)))


def pack_kernel(x_ref, g_ref, out_ref, held, sems):
    mine = pl.ds(pl.multiple_of(lax.axis_index("section") * LANES, LANES), LANES)
    copies = [pltpu.make_async_copy(ref, held.at[part], sems.at[part]) for part, ref in enumerate((x_ref, g_ref))]
    for copy in copies:
        copy.start()
    for part, copy in enumerate(copies):
        copy.wait()
        for z in range(SHARDS):
            out_ref[z, pl.ds(part * ROWS, ROWS), :] = held[part, z % 2, :, mine]


def halves_kernel(short_hbm, long_hbm, skip_hbm, gain_hbm, own_ref, send_ref, short_ref, long_ref, skip_ref, gain_ref, sems):
    section = lax.axis_index("section")
    mine = pl.ds(pl.multiple_of(section * LANES, LANES), LANES)
    other = pl.ds(pl.multiple_of((1 - section) * LANES, LANES), LANES)
    pairs = ((short_hbm, short_ref), (long_hbm, long_ref), (skip_hbm, skip_ref), (gain_hbm, gain_ref))
    copies = [pltpu.make_async_copy(a, b, sems.at[k]) for k, (a, b) in enumerate(pairs)]
    for copy in copies:
        copy.start()
    for copy in copies:
        copy.wait()
    for ref, half in ((own_ref, mine), (send_ref, other)):
        ref[pl.ds(0, KL), :] = long_ref[0, :, half]
        for i in range(3):
            for j in range(KS):
                ref[pl.ds(KL + KS * i + j, 1), :] = short_ref[i, j, :, half]
        ref[pl.ds(KL + 3 * KS, 1), :] = skip_ref[:, half]
        ref[pl.ds(KL + 3 * KS + 1, 1), :] = gain_ref[:, half]
        ref[pl.ds(PARAMS - 1, 1), :] = jnp.zeros((1, LANES), f32)


def spread(own_ref, other_ref, layer, taps):
    mine = lax.axis_index("section") == layer

    def rows_at(g):
        at = pl.ds(pl.multiple_of(g * 8, 8), 8)
        rows = jnp.where(mine, own_ref[at, :], other_ref[at, :])
        return [jnp.broadcast_to(rows[k : k + 1], (8, LANES)) for k in range(8)]

    @pl.loop(0, KL // 8)
    def _(g):
        rows = rows_at(g)
        for half in range(2):
            a, b, c, d = rows[4 * half : 4 * half + 4]
            parts = (a + b + (c + d), a + b, c + d, a + c, a, c, b + d, b, d)
            for u, part in enumerate(parts):
                taps[32 * u + 2 * g + half] = part

    for g in range(3):
        for k, row in enumerate(rows_at(KL // 8 + g)):
            taps[SHORT_AT + 8 * g + k] = row


def spread_kernel(own_ref, other_ref, taps0, token_ref):
    spread(own_ref, other_ref, 0, taps0)
    token_ref[...] = jnp.zeros_like(token_ref)


def open_kernel(in_ref, token_ref, x_ref, g_ref, out_ref, wide):
    unpack(in_ref, 0, wide, x_ref)

    def chunk(b):
        x = x_ref[pl.ds(16 * b, 16)].reshape(LANES, LANES)
        return x * x

    send_sums(out_ref, chunk)
    unpack(in_ref, 1, wide, g_ref)


def unpack(in_ref, part, wide, ref):
    for z in range(SHARDS):
        wide[pl.ds(z * ROWS, ROWS), :] = in_ref[z, pl.ds(part * ROWS, ROWS), :].astype(f32)
    for v in range(ROWS):
        ref[v] = wide[pl.ds(v, SHARDS, stride=ROWS), :]


def first_kernel(
    width, x_ref, sums_ref, taps,
    x1_ref, q_ref, mixed_ref, normed_part, f_part, k_part, v_part, scaled_part, out_ref,
    mixed, normed, scale_ref, f_ref, k_ref, v_ref, signals, results
):
    scale_and_norm(width, x_ref, sums_ref, taps, scale_ref, normed)
    forward(taps, normed, mixed, signals, results, q_ref, k_ref, v_ref, f_ref)

    def chunk(b):
        at = pl.ds(16 * b, 16)
        x1 = rounded(x_ref[at] + q_ref[at] * f_ref[at])
        x1 = x1.reshape(LANES, LANES)
        x1_ref[pl.ds(LANES * b, LANES), :] = x1.astype(bf16)
        return x1 * x1

    send_sums(out_ref, chunk)
    mixed_ref[...] = flat(mixed[pl.ds(128, ROWS)])
    start = (lax.axis_index("seq") // 2) * QUARTER
    for ref, part in ((f_ref, f_part), (k_ref, k_part), (v_ref, v_part)):
        extend_after(ref, 1)
        part[...] = ref[pl.ds(start, QUARTER + 8)]
    normed_part[...] = normed[pl.ds(start, QUARTER + 8)]
    at = pl.ds(start, QUARTER)
    scaled_part[...] = x_ref[at] * scale_ref[at]


def second_kernel(
    width, x_ref, g_ref, sums_ref, own_ref, other_ref,
    base_ref, cubes_ref, after_ref, mixed_ref, grads_ref, out_ref,
    normed, mixed, after, sq, sk, sv, q_ref, k_ref, v_ref, f_ref, scale_ref, d_ref, signals, results, taps, parts, sem
):
    spread(own_ref, other_ref, 1, taps)
    scale_rows = scale_and_norm(width, x_ref, sums_ref, taps, scale_ref, normed)
    cubes_ref[...] = scale_rows * scale_rows * scale_rows * (1.0 / width)
    forward(taps, normed, mixed, signals, results, q_ref, k_ref, v_ref, f_ref)

    @pl.loop(0, ROWS // 8)
    def _(b):
        at = pl.ds(b * 8, 8)
        e = g_ref[at]
        sq[at] = rounded(e * f_ref[at])
        d_filtered = rounded(e * q_ref[at])
        after[at] = d_filtered

    extend_after(after, 17)

    split(after, 0, signals, STRAIGHT, 6)
    convolve(taps, signals, results, False, 16)
    skip = taps[SKIP_AT][None]
    for half in range(2):
        at = pl.ds(32 * half, 32)
        d_mixed = skip * after[at] + joined(results, STRAIGHT, 8 * half, 8)
        sk[at] = rounded(d_mixed * v_ref[at])
        sv[at] = rounded(d_mixed * k_ref[at])

    for ref in (sq, sk, sv):
        extend_after(ref, 1)

    gain = taps[GAIN_AT][None]

    @pl.loop(0, ROWS // 8)
    def _(b):
        at = pl.ds(b * 8, 8)
        d_normed = normed_cotangent(taps, (sq, sk, sv), b * 8)
        k_ref[at] = d_normed
        d_ref[at] = gain * d_normed * rows_of(x_ref, b)

    def chunk(b):
        return d_ref[pl.ds(16 * b, 16)].reshape(LANES, LANES)

    send_sums(parts, chunk)
    copy = pltpu.make_async_copy(parts, out_ref, sem)
    copy.start()

    @pl.loop(0, ROWS // 8)
    def _(b):
        at = pl.ds(b * 8, 8)
        base_ref[at] = g_ref[at] + scale_ref[at] * gain * k_ref[at]

    mixed_ref[...] = flat(mixed[pl.ds(128, ROWS)])
    after_ref[...] = flat(after[pl.ds(0, ROWS)])
    start = (lax.axis_index("seq") // 2) * QUARTER
    at = pl.ds(start, QUARTER)
    sums_of_rows(
        grads_ref, (sq, sk, sv), start, normed[pl.ds(start, QUARTER + 8)],
        after[at] * mixed[pl.ds(128 + start, QUARTER)],
        jnp.sum(k_ref[at] * sixteen_of(x_ref, start // QUARTER) * scale_ref[at], axis=0),
    )
    copy.wait()


def aside_kernel(after_ref, mixed1_ref, mixed0_ref, own_ref, other_ref, grads_ref, window0, taps, window1, after):
    q = lax.axis_index("seq") // 2
    window_before(mixed1_ref, q, window1)

    @pl.loop(0, ROWS // 8)
    def _(b):
        after[pl.ds(b * 8, 8)] = rows_of(after_ref, b)

    long_sums(grads_ref, 0, after, window1)
    window_before(mixed0_ref, q, window0)
    spread(own_ref, other_ref, 0, taps)


def third_kernel(
    base_ref, x1_ref, cubes_ref, sums_ref, taps, window, scaled_part, normed_part, mixed_ref, q_ref, f_part, k_part, v_part,
    short1_ref, long1_ref, out_ref, after, errors, sq, sk, sv, grads, signals, results
):
    q = lax.axis_index("seq") // 2
    total = jnp.sum(sums_ref[...], axis=0) * cubes_ref[...]
    diagonal = eye()
    for b in range(4):
        at = pl.ds(16 * b, 16)
        e = rounded(base_ref[at] - sixteen_of(x1_ref, b) * column_of(total[b : b + 1], diagonal))
        errors[at] = e
        after[at] = rounded(e * q_ref[at])
    extend_after(after, 17)
    extend_after(errors, 1)
    start = q * QUARTER

    split(after, start, signals, STRAIGHT, 5)
    convolve(taps, signals, results, False, 6)
    at = pl.ds(start, QUARTER + 8)
    d_mixed = taps[SKIP_AT][None] * after[at] + joined(results, STRAIGHT, 0, 6)
    sq[at] = rounded(errors[at] * f_part[...])
    sk[at] = rounded(d_mixed * v_part[...])
    sv[at] = rounded(d_mixed * k_part[...])

    gain_term = jnp.zeros((SHARDS, LANES), f32)
    for b in range(2):
        d_normed = normed_cotangent(taps, (sq, sk, sv), start + 8 * b)
        gain_term = gain_term + jnp.sum(d_normed * scaled_part[pl.ds(8 * b, 8)], axis=0)
    product = after[pl.ds(start, QUARTER)] * sixteen_of(mixed_ref, q)
    sums_of_rows(grads, (sq, sk, sv), start, normed_part[...], product, gain_term)
    long_sums(grads, SHORT_ROWS, after, window)
    message0 = grads[...].astype(bf16)
    message1 = jnp.concatenate([short1_ref[...], long1_ref[...]], axis=0).astype(bf16)
    for z in range(SHARDS):
        out_ref[z] = message0
        out_ref[SHARDS + z] = message1


def close_kernel(in_ref, out_ref, whole, sems):
    sums = [None, None]
    copies = []

    def leave(first, count):
        at = pl.ds(first, count)
        copies.append(pltpu.make_async_copy(whole.at[at], out_ref.at[at], sems.at[len(copies)]))
        copies[-1].start()

    for q in range(4):
        for half in range(2):
            lanes = pl.ds(half * LANES, LANES)
            pair = in_ref[half * SHARDS + 2 * q].astype(f32) + in_ref[half * SHARDS + 2 * q + 1].astype(f32)
            whole[pl.ds(3 * KS + 32 * q, 32), 0, lanes] = pair[SHORT_ROWS:]
            sums[half] = pair[:SHORT_ROWS] if q == 0 else sums[half] + pair[:SHORT_ROWS]
        leave(3 * KS + 32 * q, 32)
    for half in range(2):
        lanes = pl.ds(half * LANES, LANES)
        whole[pl.ds(0, 3 * KS), 0, lanes] = sums[half][: 3 * KS]
        whole[pl.ds(3 * KS + KL, 2), 0, lanes] = sums[half][3 * KS : 3 * KS + 2]
    leave(0, 3 * KS)
    leave(3 * KS + KL, 2)
    for copy in copies:
        copy.wait()


VMEM = pl.BlockSpec(memory_space=pltpu.VMEM)
HBM = pl.BlockSpec(memory_space=pltpu.HBM)


def call(kernel, name, outs, operands, scratch=(), ins=VMEM, in_hbm=None, flops=0):
    cost = pl.CostEstimate(flops=flops, bytes_accessed=0, transcendentals=0) if flops else None
    return pl.pallas_call(
        kernel,
        name=name,
        out_shape=[jax.ShapeDtypeStruct(shape, dtype) for shape, dtype in outs],
        in_specs=[ins] * len(operands),
        out_specs=[HBM if i == in_hbm else VMEM for i in range(len(outs))],
        scratch_shapes=[s if not isinstance(s, tuple) else pltpu.VMEM(*s) for s in scratch],
        cost_estimate=cost,
        compiler_params=pltpu.CompilerParams(vmem_limit_bytes=20 * 1024 * 1024),
    )(*operands)


def block(rows):
    return ((rows, SHARDS, LANES), f32)


def on_device(inputs, out_grad, short_filters, long_filters, skip_gain, norm_gain):
    chan = lax.axis_size("chan")
    width = chan * inputs.shape[2]
    params = ((PARAMS, LANES), f32)
    sums = ((2 * chan, 4, LANES), f32)
    wide = ((SHARDS * ROWS, LANES), f32)
    rows, longer, thrice, taps, part_rows = block(ROWS), block(ROWS + 8), block(200), block(TAPS), block(QUARTER + 8)
    splits = [((PARTS, 48, SHARDS, LANES), f32), ((PARTS, 16, SHARDS, LANES), f32)]
    kept = ((SHARDS * ROWS, LANES), bf16)
    shorts, longs = ((SHORT_ROWS, LANES), f32), ((32, LANES), f32)

    (packed,) = call(
        pack_kernel, "pack", [((SHARDS, 2 * ROWS, LANES), bf16)],
        tuple(pltpu.with_memory_space_constraint(a, pltpu.HBM) for a in (inputs, out_grad)),
        [((2, 2, ROWS, 2 * LANES), bf16), pltpu.SemaphoreType.DMA((2,))], HBM,
    )
    arrived = lax.all_to_all(packed, "seq", 0, 0)
    stored = (short_filters.transpose(1, 2, 0, 3), long_filters, skip_gain, norm_gain)
    own, send = call(
        halves_kernel, "halves", [params] * 2, tuple(pltpu.with_memory_space_constraint(a, pltpu.HBM) for a in stored),
        [(a.shape, f32) for a in stored] + [pltpu.SemaphoreType.DMA((4,))], HBM,
    )
    other = lax.ppermute(send, "section", [(0, 1), (1, 0)])
    taps0, token = call(spread_kernel, "spread", [taps, block(1)], (own, other))
    x0, g, part = call(open_kernel, "open", [rows, rows, sums], (arrived, token), [wide])

    def over_channels(part):
        return lax.all_to_all(part, ("section", "chan"), 0, 0)

    x1, q0, mixed0, normed0, f0, k0, v0, scaled0, part = call(
        functools.partial(first_kernel, width), "first",
        [kept, rows, kept] + [part_rows] * 4 + [block(QUARTER), sums], (x0, over_channels(part), taps0),
        [thrice, longer, rows, longer, longer, longer] + splits,
    )
    base, cubes, after1, mixed1, short1, part = call(
        functools.partial(second_kernel, width), "second",
        [rows, ((4, LANES), f32), kept, kept, shorts, sums], (x1, g, over_channels(part), own, other),
        [longer, thrice, thrice] + [longer] * 3 + [rows] * 6 + splits + [taps, sums, pltpu.SemaphoreType.DMA], in_hbm=5,
    )
    all_part = over_channels(part)
    long1, window0, taps0 = call(
        aside_kernel, "aside", [longs, block(112), taps], (after1, mixed1, mixed0, own, other), [block(112), rows],
        flops=2000000,
    )
    (message,) = call(
        third_kernel, "third", [((2 * SHARDS, MESSAGE, LANES), bf16)],
        (base, x1, cubes, all_part, taps0, window0, scaled0, normed0, mixed0, q0, f0, k0, v0, short1, long1),
        [block(216)] + [longer] * 4 + [((MESSAGE, LANES), f32)] + splits,
    )
    gathered = lax.all_to_all(message, ("section", "seq"), 0, 0)
    result = ((3 * KS + KL + 2, 1, 2 * LANES), f32)
    (grads,) = call(close_kernel, "close", [result], (gathered,), [result, pltpu.SemaphoreType.DMA((6,))], in_hbm=0)
    return grads.transpose(1, 0, 2)


def solution(mesh):
    placed = (
        P(None, "seq", "chan"),
        P(None, "seq", "chan"),
        P("section", None, None, "chan"),
        P("section", None, "chan"),
        P("section", "chan"),
        P("section", "chan"),
    )
    return jax.shard_map(
        on_device, mesh=mesh, in_specs=placed, out_specs=P("section", None, "chan"), check_vma=False
    )
```

```python
import functools

import jax
import jax.numpy as jnp
from jax import lax
from jax.experimental import pallas as pl
from jax.experimental.pallas import tpu as pltpu
from jax.sharding import PartitionSpec as P

EPSILON = 1e-06
SHARDS = 8
ROWS = 64
LANES = 128
KS = 7
KL = 128
PARAMS = 152
UNROLLED = 3
PARTS = 9
SHORT_AT, SKIP_AT, GAIN_AT, TAPS = 288, 309, 310, 312
QUARTER = ROWS // 4
SHORT_ROWS = 32
MESSAGE = SHORT_ROWS + 32
f32 = jnp.float32
bf16 = jnp.bfloat16


def rounded(a):
    return a.astype(bf16).astype(f32)


def later(a, count):
    sub = lax.broadcasted_iota(jnp.int32, a.shape, 1)
    return jnp.where(sub >= count, pltpu.roll(a, count, 1), 0.0)


def sooner(a, count):
    sub = lax.broadcasted_iota(jnp.int32, a.shape, 1)
    return jnp.where(sub < SHARDS - count, pltpu.roll(a, SHARDS - count, 1), 0.0)


def eye():
    shape = (LANES, LANES)
    return lax.broadcasted_iota(jnp.int32, shape, 0) == lax.broadcasted_iota(jnp.int32, shape, 1)


def send_sums(out_ref, chunk_of):
    diagonal = eye()
    rows = []
    for b in range(4):
        column = jnp.sum(chunk_of(b), axis=1, keepdims=True)
        rows.append(jnp.sum(jnp.where(diagonal, column, 0.0), axis=0, keepdims=True))
    whole = jnp.concatenate(rows, axis=0)
    out_ref[...] = jnp.broadcast_to(whole[None], out_ref.shape)


def column_of(row, diagonal):
    column = jnp.sum(jnp.where(diagonal, row, 0.0), axis=1, keepdims=True)
    return jnp.broadcast_to(column, (LANES, LANES)).reshape(16, SHARDS, LANES)


def sixteen_of(ref, b):
    if len(ref.shape) == 3:
        return ref[pl.ds(16 * b, 16)]
    at = pl.ds(pl.multiple_of(b * LANES, LANES), LANES)
    return ref[at, :].astype(f32).reshape(16, SHARDS, LANES)


def scale_and_norm(width, x_ref, sums_ref, taps, scale_ref, normed):
    total = jnp.sum(sums_ref[...], axis=0)
    scale_rows = lax.rsqrt(total * (1.0 / width) + EPSILON)
    diagonal = eye()
    gain = taps[GAIN_AT]
    for b in range(4):
        scale = column_of(scale_rows[b : b + 1], diagonal)
        scale_ref[pl.ds(16 * b, 16)] = scale
        normed[pl.ds(8 + 16 * b, 16)] = rounded(sixteen_of(x_ref, b) * scale * gain[None])
    normed[pl.ds(0, 8)] = later(normed[pl.ds(64, 8)], 1)
    return scale_rows


def forward(taps, normed, mixed, signals, results, q_ref, k_ref, v_ref, f_ref):
    @pl.loop(0, ROWS // 8)
    def _(b):
        near = normed[pl.ds(b * 8, 16)]
        streams = []
        for i in range(3):
            total = None
            for j in range(KS):
                term = taps[SHORT_AT + KS * i + j][None] * near[8 - j : 16 - j]
                total = term if total is None else total + term
            streams.append(total)
        at = pl.ds(b * 8, 8)
        q_ref[at] = streams[0]
        k_ref[at] = streams[1]
        v_ref[at] = streams[2]
        z = rounded(streams[1] * streams[2])
        mixed[pl.ds(128 + b * 8, 8)] = z
        mixed[pl.ds(64 + b * 8, 8)] = later(z, 1)
        mixed[pl.ds(b * 8, 8)] = later(z, 2)

    split(mixed, 1, signals, REVERSED, 6)
    convolve(taps, signals, results, True, 16)
    skip = taps[SKIP_AT][None]
    for half in range(2):
        at = pl.ds(32 * half, 32)
        f_ref[at] = skip * mixed[pl.ds(128 + 32 * half, 32)] + joined(results, REVERSED, 8 * half, 8)


def split(ref, start, signals, order, blocks):
    @pl.loop(0, blocks)
    def _(g):
        near = ref[pl.ds(start + 32 * g, 32)].reshape(8, 4, SHARDS, LANES)
        far = ref[pl.ds(start + 4 + 32 * g, 32)].reshape(8, 4, SHARDS, LANES)
        s = [near[:, 0], near[:, 1], near[:, 2], near[:, 3], far[:, 0], far[:, 1], far[:, 2]]
        one = (s[1], s[3], s[5])
        two = (s[0] - s[1], s[2] - s[3], s[4] - s[5])
        three = (s[2] - s[1], s[4] - s[3], s[6] - s[5])
        for t, (before, middle, after) in enumerate((one, two, three)):
            for p, part in enumerate((middle, before - middle, after - middle)):
                signals[order[3 * t + p], pl.ds(8 * g, 8)] = part


STRAIGHT = (0, 1, 2, 3, 4, 5, 6, 7, 8)
REVERSED = (0, 2, 1, 6, 8, 7, 3, 5, 4)


def convolve(taps, signals, results, backwards, count):
    @pl.loop(0, PARTS // UNROLLED)
    def _(several):
        for one in range(UNROLLED):
            u = several * UNROLLED + one
            total = jnp.zeros((count, SHARDS, LANES), f32)
            for g in range(2):
                z = signals[u, pl.ds(16 * g, count + 15)]
                w = taps[pl.ds(32 * u + 16 * (1 - g if backwards else g), 16)]
                for a in range(16):
                    total = total + w[15 - a if backwards else a][None] * z[a : a + count]
            results[u, pl.ds(0, count)] = total


def joined(results, order, start, count):
    even, odd = [], []
    for t in range(3):
        middle, first, last = (results[order[3 * t + p], pl.ds(start, count)] for p in range(3))
        even.append(middle + first)
        odd.append(middle + last)
    rows = [even[0] + even[1], even[0] + even[2], odd[0] + odd[1], odd[0] + odd[2]]
    return jnp.stack(rows, axis=1).reshape(4 * count, SHARDS, LANES)


def extend_after(ref, blocks):
    if blocks == 1:
        ref[pl.ds(64, 8)] = sooner(ref[pl.ds(0, 8)], 1)
        return

    @pl.loop(0, 8)
    def _(b):
        a = ref[pl.ds(b * 8, 8)]
        ref[pl.ds(64 + b * 8, 8)] = sooner(a, 1)
        ref[pl.ds(128 + b * 8, 8)] = sooner(a, 2)

    ref[pl.ds(192, 8)] = sooner(ref[pl.ds(0, 8)], 3)


def normed_cotangent(taps, streams, start):
    total = None
    for i in range(3):
        near = streams[i][pl.ds(start, 16)]
        for j in range(KS):
            term = taps[SHORT_AT + KS * i + j][None] * near[j : j + 8]
            total = term if total is None else total + term
    return total


def over_shards(a):
    return jnp.sum(a, axis=1)


def sums_of_rows(out_ref, streams, start, near, product, gain_term):
    rows = []
    for i in range(3):
        stream = streams[i][pl.ds(start, QUARTER)]
        for j in range(KS):
            rows.append(jnp.sum(stream * near[8 - j : 8 - j + QUARTER], axis=0))
    rows.append(jnp.sum(product, axis=0))
    rows.append(gain_term)
    while len(rows) < SHORT_ROWS:
        rows.append(jnp.zeros((SHARDS, LANES), f32))
    out_ref[pl.ds(0, SHORT_ROWS), :] = over_shards(jnp.stack(rows, axis=0))


def long_sums(out_ref, at, after, window):
    for half in range(2):
        sums = [None] * 16
        for b in range(ROWS // 16):
            d = after[pl.ds(b * 16, 16)]
            z = window[pl.ds(17 + 16 * (b - half), 31)]
            for a in range(16):
                term = jnp.sum(d * z[15 - a : 31 - a], axis=0)
                sums[a] = term if b == 0 else sums[a] + term
        out_ref[pl.ds(at + half * 16, 16), :] = over_shards(jnp.stack(sums, axis=0))


def flat(a):
    return a.reshape(ROWS * SHARDS, LANES).astype(bf16)


def rows_of(ref, b):
    at = pl.ds(pl.multiple_of(b * 64, 64), 64)
    return ref[at, :].astype(f32).reshape(8, SHARDS, LANES)


def window_before(own_ref, q, window):
    @pl.loop(0, 14)
    def _(b):
        block = 12 - 4 * q + b
        z = rows_of(own_ref, block % 8)
        back = block // 8
        window[pl.ds(8 * b, 8)] = jnp.where(back == 2, z, jnp.where(back == 1, later(z, 1), later(z, 2)))


def pack_kernel(x_ref, g_ref, out_ref, held, sems):
    mine = pl.ds(pl.multiple_of(lax.axis_index("section") * LANES, LANES), LANES)
    copies = [pltpu.make_async_copy(ref, held.at[part], sems.at[part]) for part, ref in enumerate((x_ref, g_ref))]
    for copy in copies:
        copy.start()
    for part, copy in enumerate(copies):
        copy.wait()
        for z in range(SHARDS):
            out_ref[z, pl.ds(part * ROWS, ROWS), :] = held[part, z % 2, :, mine]


def halves_kernel(short_hbm, long_hbm, skip_hbm, gain_hbm, own_ref, send_ref, short_ref, long_ref, skip_ref, gain_ref, sems):
    section = lax.axis_index("section")
    mine = pl.ds(pl.multiple_of(section * LANES, LANES), LANES)
    other = pl.ds(pl.multiple_of((1 - section) * LANES, LANES), LANES)
    pairs = ((short_hbm, short_ref), (long_hbm, long_ref), (skip_hbm, skip_ref), (gain_hbm, gain_ref))
    copies = [pltpu.make_async_copy(a, b, sems.at[k]) for k, (a, b) in enumerate(pairs)]
    for copy in copies:
        copy.start()
    for copy in copies:
        copy.wait()
    for ref, half in ((own_ref, mine), (send_ref, other)):
        ref[pl.ds(0, KL), :] = long_ref[0, :, half]
        for i in range(3):
            for j in range(KS):
                ref[pl.ds(KL + KS * i + j, 1), :] = short_ref[i, j, :, half]
        ref[pl.ds(KL + 3 * KS, 1), :] = skip_ref[:, half]
        ref[pl.ds(KL + 3 * KS + 1, 1), :] = gain_ref[:, half]
        ref[pl.ds(PARAMS - 1, 1), :] = jnp.zeros((1, LANES), f32)


def spread(own_ref, other_ref, layer, taps):
    mine = lax.axis_index("section") == layer

    def rows_at(g):
        at = pl.ds(pl.multiple_of(g * 8, 8), 8)
        rows = jnp.where(mine, own_ref[at, :], other_ref[at, :])
        return [jnp.broadcast_to(rows[k : k + 1], (8, LANES)) for k in range(8)]

    @pl.loop(0, KL // 8)
    def _(g):
        rows = rows_at(g)
        for half in range(2):
            a, b, c, d = rows[4 * half : 4 * half + 4]
            parts = (a + b + (c + d), a + b, c + d, a + c, a, c, b + d, b, d)
            for u, part in enumerate(parts):
                taps[32 * u + 2 * g + half] = part

    for g in range(3):
        for k, row in enumerate(rows_at(KL // 8 + g)):
            taps[SHORT_AT + 8 * g + k] = row


def spread_kernel(own_ref, other_ref, taps0, token_ref):
    spread(own_ref, other_ref, 0, taps0)
    token_ref[...] = jnp.zeros_like(token_ref)


def open_kernel(in_ref, token_ref, x_ref, g_ref, out_ref, wide):
    unpack(in_ref, 0, wide, x_ref)

    def chunk(b):
        x = x_ref[pl.ds(16 * b, 16)].reshape(LANES, LANES)
        return x * x

    send_sums(out_ref, chunk)
    unpack(in_ref, 1, wide, g_ref)


def unpack(in_ref, part, wide, ref):
    for z in range(SHARDS):
        wide[pl.ds(z * ROWS, ROWS), :] = in_ref[z, pl.ds(part * ROWS, ROWS), :].astype(f32)
    for v in range(ROWS):
        ref[v] = wide[pl.ds(v, SHARDS, stride=ROWS), :]


def first_kernel(
    width, x_ref, sums_ref, taps,
    x1_ref, q_ref, mixed_ref, normed_part, f_part, k_part, v_part, scaled_part, out_ref,
    mixed, normed, scale_ref, f_ref, k_ref, v_ref, signals, results
):
    scale_and_norm(width, x_ref, sums_ref, taps, scale_ref, normed)
    forward(taps, normed, mixed, signals, results, q_ref, k_ref, v_ref, f_ref)

    def chunk(b):
        at = pl.ds(16 * b, 16)
        x1 = rounded(x_ref[at] + q_ref[at] * f_ref[at])
        x1 = x1.reshape(LANES, LANES)
        x1_ref[pl.ds(LANES * b, LANES), :] = x1.astype(bf16)
        return x1 * x1

    send_sums(out_ref, chunk)
    mixed_ref[...] = flat(mixed[pl.ds(128, ROWS)])
    start = (lax.axis_index("seq") // 2) * QUARTER
    for ref, part in ((f_ref, f_part), (k_ref, k_part), (v_ref, v_part)):
        extend_after(ref, 1)
        part[...] = ref[pl.ds(start, QUARTER + 8)]
    normed_part[...] = normed[pl.ds(start, QUARTER + 8)]
    at = pl.ds(start, QUARTER)
    scaled_part[...] = x_ref[at] * scale_ref[at]


def second_kernel(
    width, x_ref, g_ref, sums_ref, own_ref, other_ref,
    base_ref, cubes_ref, after_ref, mixed_ref, grads_ref, out_ref,
    normed, mixed, after, sq, sk, sv, q_ref, k_ref, v_ref, f_ref, scale_ref, d_ref, signals, results, taps, parts, sem
):
    spread(own_ref, other_ref, 1, taps)
    scale_rows = scale_and_norm(width, x_ref, sums_ref, taps, scale_ref, normed)
    cubes_ref[...] = scale_rows * scale_rows * scale_rows * (1.0 / width)
    forward(taps, normed, mixed, signals, results, q_ref, k_ref, v_ref, f_ref)

    @pl.loop(0, ROWS // 8)
    def _(b):
        at = pl.ds(b * 8, 8)
        e = g_ref[at]
        sq[at] = rounded(e * f_ref[at])
        d_filtered = rounded(e * q_ref[at])
        after[at] = d_filtered

    extend_after(after, 17)

    split(after, 0, signals, STRAIGHT, 6)
    convolve(taps, signals, results, False, 16)
    skip = taps[SKIP_AT][None]
    for half in range(2):
        at = pl.ds(32 * half, 32)
        d_mixed = skip * after[at] + joined(results, STRAIGHT, 8 * half, 8)
        sk[at] = rounded(d_mixed * v_ref[at])
        sv[at] = rounded(d_mixed * k_ref[at])

    for ref in (sq, sk, sv):
        extend_after(ref, 1)

    gain = taps[GAIN_AT][None]

    @pl.loop(0, ROWS // 8)
    def _(b):
        at = pl.ds(b * 8, 8)
        d_normed = normed_cotangent(taps, (sq, sk, sv), b * 8)
        k_ref[at] = d_normed
        d_ref[at] = gain * d_normed * rows_of(x_ref, b)

    def chunk(b):
        return d_ref[pl.ds(16 * b, 16)].reshape(LANES, LANES)

    send_sums(parts, chunk)
    copy = pltpu.make_async_copy(parts, out_ref, sem)
    copy.start()

    @pl.loop(0, ROWS // 8)
    def _(b):
        at = pl.ds(b * 8, 8)
        base_ref[at] = g_ref[at] + scale_ref[at] * gain * k_ref[at]

    mixed_ref[...] = flat(mixed[pl.ds(128, ROWS)])
    after_ref[...] = flat(after[pl.ds(0, ROWS)])
    start = (lax.axis_index("seq") // 2) * QUARTER
    at = pl.ds(start, QUARTER)
    sums_of_rows(
        grads_ref, (sq, sk, sv), start, normed[pl.ds(start, QUARTER + 8)],
        after[at] * mixed[pl.ds(128 + start, QUARTER)],
        jnp.sum(k_ref[at] * sixteen_of(x_ref, start // QUARTER) * scale_ref[at], axis=0),
    )
    copy.wait()


def aside_kernel(after_ref, mixed1_ref, mixed0_ref, own_ref, other_ref, grads_ref, window0, taps, window1, after):
    q = lax.axis_index("seq") // 2
    window_before(mixed1_ref, q, window1)

    @pl.loop(0, ROWS // 8)
    def _(b):
        after[pl.ds(b * 8, 8)] = rows_of(after_ref, b)

    long_sums(grads_ref, 0, after, window1)
    window_before(mixed0_ref, q, window0)
    spread(own_ref, other_ref, 0, taps)


def third_kernel(
    base_ref, x1_ref, cubes_ref, sums_ref, taps, window, scaled_part, normed_part, mixed_ref, q_ref, f_part, k_part, v_part,
    short1_ref, long1_ref, out_ref, after, errors, sq, sk, sv, grads, signals, results
):
    q = lax.axis_index("seq") // 2
    total = jnp.sum(sums_ref[...], axis=0) * cubes_ref[...]
    diagonal = eye()
    for b in range(4):
        at = pl.ds(16 * b, 16)
        e = rounded(base_ref[at] - sixteen_of(x1_ref, b) * column_of(total[b : b + 1], diagonal))
        errors[at] = e
        after[at] = rounded(e * q_ref[at])
    extend_after(after, 17)
    extend_after(errors, 1)
    start = q * QUARTER

    split(after, start, signals, STRAIGHT, 5)
    convolve(taps, signals, results, False, 6)
    at = pl.ds(start, QUARTER + 8)
    d_mixed = taps[SKIP_AT][None] * after[at] + joined(results, STRAIGHT, 0, 6)
    sq[at] = rounded(errors[at] * f_part[...])
    sk[at] = rounded(d_mixed * v_part[...])
    sv[at] = rounded(d_mixed * k_part[...])

    gain_term = jnp.zeros((SHARDS, LANES), f32)
    for b in range(2):
        d_normed = normed_cotangent(taps, (sq, sk, sv), start + 8 * b)
        gain_term = gain_term + jnp.sum(d_normed * scaled_part[pl.ds(8 * b, 8)], axis=0)
    product = after[pl.ds(start, QUARTER)] * sixteen_of(mixed_ref, q)
    sums_of_rows(grads, (sq, sk, sv), start, normed_part[...], product, gain_term)
    long_sums(grads, SHORT_ROWS, after, window)
    message0 = grads[...].astype(bf16)
    message1 = jnp.concatenate([short1_ref[...], long1_ref[...]], axis=0).astype(bf16)
    for z in range(SHARDS):
        out_ref[z] = message0
        out_ref[SHARDS + z] = message1


def close_kernel(in_ref, out_ref, whole, sems):
    sums = [None, None]
    copies = []

    def leave(first, count):
        at = pl.ds(first, count)
        copies.append(pltpu.make_async_copy(whole.at[at], out_ref.at[at], sems.at[len(copies)]))
        copies[-1].start()

    for q in range(4):
        for half in range(2):
            lanes = pl.ds(half * LANES, LANES)
            pair = in_ref[half * SHARDS + 2 * q].astype(f32) + in_ref[half * SHARDS + 2 * q + 1].astype(f32)
            whole[pl.ds(3 * KS + 32 * q, 32), 0, lanes] = pair[SHORT_ROWS:]
            sums[half] = pair[:SHORT_ROWS] if q == 0 else sums[half] + pair[:SHORT_ROWS]
        leave(3 * KS + 32 * q, 32)
    for half in range(2):
        lanes = pl.ds(half * LANES, LANES)
        whole[pl.ds(0, 3 * KS), 0, lanes] = sums[half][: 3 * KS]
        whole[pl.ds(3 * KS + KL, 2), 0, lanes] = sums[half][3 * KS : 3 * KS + 2]
    leave(0, 3 * KS)
    leave(3 * KS + KL, 2)
    for copy in copies:
        copy.wait()


VMEM = pl.BlockSpec(memory_space=pltpu.VMEM)
HBM = pl.BlockSpec(memory_space=pltpu.HBM)


def call(kernel, name, outs, operands, scratch=(), ins=VMEM, in_hbm=None, flops=0):
    cost = pl.CostEstimate(flops=flops, bytes_accessed=0, transcendentals=0) if flops else None
    return pl.pallas_call(
        kernel,
        name=name,
        out_shape=[jax.ShapeDtypeStruct(shape, dtype) for shape, dtype in outs],
        in_specs=[ins] * len(operands),
        out_specs=[HBM if i == in_hbm else VMEM for i in range(len(outs))],
        scratch_shapes=[s if not isinstance(s, tuple) else pltpu.VMEM(*s) for s in scratch],
        cost_estimate=cost,
        compiler_params=pltpu.CompilerParams(vmem_limit_bytes=20 * 1024 * 1024),
    )(*operands)


def block(rows):
    return ((rows, SHARDS, LANES), f32)


def on_device(inputs, out_grad, short_filters, long_filters, skip_gain, norm_gain):
    chan = lax.axis_size("chan")
    width = chan * inputs.shape[2]
    params = ((PARAMS, LANES), f32)
    sums = ((2 * chan, 4, LANES), f32)
    wide = ((SHARDS * ROWS, LANES), f32)
    rows, longer, thrice, taps, part_rows = block(ROWS), block(ROWS + 8), block(200), block(TAPS), block(QUARTER + 8)
    splits = [((PARTS, 48, SHARDS, LANES), f32), ((PARTS, 16, SHARDS, LANES), f32)]
    kept = ((SHARDS * ROWS, LANES), bf16)
    shorts, longs = ((SHORT_ROWS, LANES), f32), ((32, LANES), f32)

    (packed,) = call(
        pack_kernel, "pack", [((SHARDS, 2 * ROWS, LANES), bf16)],
        tuple(pltpu.with_memory_space_constraint(a, pltpu.HBM) for a in (inputs, out_grad)),
        [((2, 2, ROWS, 2 * LANES), bf16), pltpu.SemaphoreType.DMA((2,))], HBM,
    )
    arrived = lax.all_to_all(packed, "seq", 0, 0)
    stored = (short_filters.transpose(1, 2, 0, 3), long_filters, skip_gain, norm_gain)
    own, send = call(
        halves_kernel, "halves", [params] * 2, tuple(pltpu.with_memory_space_constraint(a, pltpu.HBM) for a in stored),
        [(a.shape, f32) for a in stored] + [pltpu.SemaphoreType.DMA((4,))], HBM,
    )
    other = lax.ppermute(send, "section", [(0, 1), (1, 0)])
    taps0, token = call(spread_kernel, "spread", [taps, block(1)], (own, other))
    x0, g, part = call(open_kernel, "open", [rows, rows, sums], (arrived, token), [wide])

    def over_channels(part):
        return lax.all_to_all(part, ("section", "chan"), 0, 0)

    x1, q0, mixed0, normed0, f0, k0, v0, scaled0, part = call(
        functools.partial(first_kernel, width), "first",
        [kept, rows, kept] + [part_rows] * 4 + [block(QUARTER), sums], (x0, over_channels(part), taps0),
        [thrice, longer, rows, longer, longer, longer] + splits,
    )
    base, cubes, after1, mixed1, short1, part = call(
        functools.partial(second_kernel, width), "second",
        [rows, ((4, LANES), f32), kept, kept, shorts, sums], (x1, g, over_channels(part), own, other),
        [longer, thrice, thrice] + [longer] * 3 + [rows] * 6 + splits + [taps, sums, pltpu.SemaphoreType.DMA], in_hbm=5,
    )
    all_part = over_channels(part)
    long1, window0, taps0 = call(
        aside_kernel, "aside", [longs, block(112), taps], (after1, mixed1, mixed0, own, other), [block(112), rows],
        flops=2000000,
    )
    (message,) = call(
        third_kernel, "third", [((2 * SHARDS, MESSAGE, LANES), bf16)],
        (base, x1, cubes, all_part, taps0, window0, scaled0, normed0, mixed0, q0, f0, k0, v0, short1, long1),
        [block(216)] + [longer] * 4 + [((MESSAGE, LANES), f32)] + splits,
    )
    gathered = lax.all_to_all(message, ("section", "seq"), 0, 0)
    result = ((3 * KS + KL + 2, 1, 2 * LANES), f32)
    (grads,) = call(close_kernel, "close", [result], (gathered,), [result, pltpu.SemaphoreType.DMA((6,))], in_hbm=0)
    return grads.transpose(1, 0, 2)


def solution(mesh):
    placed = (
        P(None, "seq", "chan"),
        P(None, "seq", "chan"),
        P("section", None, None, "chan"),
        P("section", None, "chan"),
        P("section", "chan"),
        P("section", "chan"),
    )
    return jax.shard_map(
        on_device, mesh=mesh, in_specs=placed, out_specs=P("section", None, "chan"), check_vma=False
    )
```

```python
import functools

import jax
import jax.numpy as jnp
from jax import lax
from jax.experimental import pallas as pl
from jax.experimental.pallas import tpu as pltpu
from jax.sharding import PartitionSpec as P

EPSILON = 1e-06
SHARDS = 8
ROWS = 64
LANES = 128
KS = 7
KL = 128
PARAMS = 152
UNROLLED = 3
PARTS = 9
SHORT_AT, SKIP_AT, GAIN_AT, TAPS = 288, 309, 310, 312
QUARTER = ROWS // 4
SHORT_ROWS = 32
MESSAGE = SHORT_ROWS + 32
f32 = jnp.float32
bf16 = jnp.bfloat16


def rounded(a):
    return a.astype(bf16).astype(f32)


def later(a, count):
    sub = lax.broadcasted_iota(jnp.int32, a.shape, 1)
    return jnp.where(sub >= count, pltpu.roll(a, count, 1), 0.0)


def sooner(a, count):
    sub = lax.broadcasted_iota(jnp.int32, a.shape, 1)
    return jnp.where(sub < SHARDS - count, pltpu.roll(a, SHARDS - count, 1), 0.0)


def eye():
    shape = (LANES, LANES)
    return lax.broadcasted_iota(jnp.int32, shape, 0) == lax.broadcasted_iota(jnp.int32, shape, 1)


def send_sums(out_ref, chunk_of):
    diagonal = eye()
    rows = []
    for b in range(4):
        column = jnp.sum(chunk_of(b), axis=1, keepdims=True)
        rows.append(jnp.sum(jnp.where(diagonal, column, 0.0), axis=0, keepdims=True))
    whole = jnp.concatenate(rows, axis=0)
    out_ref[...] = jnp.broadcast_to(whole[None], out_ref.shape)


def column_of(row, diagonal):
    column = jnp.sum(jnp.where(diagonal, row, 0.0), axis=1, keepdims=True)
    return jnp.broadcast_to(column, (LANES, LANES)).reshape(16, SHARDS, LANES)


def total_of(ref):
    parts = ref[...]
    while parts.shape[0] > 1:
        half = parts.shape[0] // 2
        parts = parts[:half] + parts[half:]
    return parts[0]


def sixteen_of(ref, b):
    if len(ref.shape) == 3:
        return ref[pl.ds(16 * b, 16)]
    at = pl.ds(pl.multiple_of(b * LANES, LANES), LANES)
    return ref[at, :].astype(f32).reshape(16, SHARDS, LANES)


def scale_and_norm(width, x_ref, sums_ref, taps, scale_ref, normed):
    total = total_of(sums_ref)
    scale_rows = lax.rsqrt(total * (1.0 / width) + EPSILON)
    diagonal = eye()
    gain = taps[GAIN_AT]
    for b in range(4):
        scale = column_of(scale_rows[b : b + 1], diagonal)
        scale_ref[pl.ds(16 * b, 16)] = scale
        normed[pl.ds(8 + 16 * b, 16)] = rounded(sixteen_of(x_ref, b) * scale * gain[None])
    normed[pl.ds(0, 8)] = later(normed[pl.ds(64, 8)], 1)
    return scale_rows


def forward(taps, normed, mixed, signals, results, q_ref, k_ref, v_ref, f_ref):
    @pl.loop(0, ROWS // 8)
    def _(b):
        near = normed[pl.ds(b * 8, 16)]
        streams = []
        for i in range(3):
            total = None
            for j in range(KS):
                term = taps[SHORT_AT + KS * i + j][None] * near[8 - j : 16 - j]
                total = term if total is None else total + term
            streams.append(total)
        at = pl.ds(b * 8, 8)
        q_ref[at] = streams[0]
        k_ref[at] = streams[1]
        v_ref[at] = streams[2]
        z = rounded(streams[1] * streams[2])
        mixed[pl.ds(128 + b * 8, 8)] = z
        mixed[pl.ds(64 + b * 8, 8)] = later(z, 1)
        mixed[pl.ds(b * 8, 8)] = later(z, 2)

    split(mixed, 1, signals, REVERSED, 6)
    convolve(taps, signals, results, True, 16)
    skip = taps[SKIP_AT][None]
    for half in range(2):
        at = pl.ds(32 * half, 32)
        f_ref[at] = skip * mixed[pl.ds(128 + 32 * half, 32)] + joined(results, REVERSED, 8 * half, 8)


def split(ref, start, signals, order, blocks):
    @pl.loop(0, blocks)
    def _(g):
        near = ref[pl.ds(start + 32 * g, 32)].reshape(8, 4, SHARDS, LANES)
        far = ref[pl.ds(start + 4 + 32 * g, 32)].reshape(8, 4, SHARDS, LANES)
        s = [near[:, 0], near[:, 1], near[:, 2], near[:, 3], far[:, 0], far[:, 1], far[:, 2]]
        one = (s[1], s[3], s[5])
        two = (s[0] - s[1], s[2] - s[3], s[4] - s[5])
        three = (s[2] - s[1], s[4] - s[3], s[6] - s[5])
        for t, (before, middle, after) in enumerate((one, two, three)):
            for p, part in enumerate((middle, before - middle, after - middle)):
                signals[order[3 * t + p], pl.ds(8 * g, 8)] = part


STRAIGHT = (0, 1, 2, 3, 4, 5, 6, 7, 8)
REVERSED = (0, 2, 1, 6, 8, 7, 3, 5, 4)


def convolve(taps, signals, results, backwards, count):
    @pl.loop(0, PARTS // UNROLLED)
    def _(several):
        for one in range(UNROLLED):
            u = several * UNROLLED + one
            total = jnp.zeros((count, SHARDS, LANES), f32)
            for g in range(2):
                z = signals[u, pl.ds(16 * g, count + 15)]
                w = taps[pl.ds(32 * u + 16 * (1 - g if backwards else g), 16)]
                for a in range(16):
                    total = total + w[15 - a if backwards else a][None] * z[a : a + count]
            results[u, pl.ds(0, count)] = total


def joined(results, order, start, count):
    even, odd = [], []
    for t in range(3):
        middle, first, last = (results[order[3 * t + p], pl.ds(start, count)] for p in range(3))
        even.append(middle + first)
        odd.append(middle + last)
    rows = [even[0] + even[1], even[0] + even[2], odd[0] + odd[1], odd[0] + odd[2]]
    return jnp.stack(rows, axis=1).reshape(4 * count, SHARDS, LANES)


def extend_after(ref, blocks):
    if blocks == 1:
        ref[pl.ds(64, 8)] = sooner(ref[pl.ds(0, 8)], 1)
        return

    @pl.loop(0, 8)
    def _(b):
        a = ref[pl.ds(b * 8, 8)]
        ref[pl.ds(64 + b * 8, 8)] = sooner(a, 1)
        ref[pl.ds(128 + b * 8, 8)] = sooner(a, 2)

    ref[pl.ds(192, 8)] = sooner(ref[pl.ds(0, 8)], 3)


def normed_cotangent(taps, streams, start):
    total = None
    for i in range(3):
        near = streams[i][pl.ds(start, 16)]
        for j in range(KS):
            term = taps[SHORT_AT + KS * i + j][None] * near[j : j + 8]
            total = term if total is None else total + term
    return total


def over_shards(a):
    return jnp.sum(a, axis=1)


def sums_of_rows(out_ref, streams, start, near, product, gain_term):
    rows = []
    for i in range(3):
        stream = streams[i][pl.ds(start, QUARTER)]
        for j in range(KS):
            rows.append(jnp.sum(stream * near[8 - j : 8 - j + QUARTER], axis=0))
    rows.append(jnp.sum(product, axis=0))
    rows.append(gain_term)
    while len(rows) < SHORT_ROWS:
        rows.append(jnp.zeros((SHARDS, LANES), f32))
    out_ref[pl.ds(0, SHORT_ROWS), :] = over_shards(jnp.stack(rows, axis=0))


def long_sums(out_ref, at, after, window):
    for half in range(2):
        sums = [None] * 16
        for b in range(ROWS // 16):
            d = after[pl.ds(b * 16, 16)]
            z = window[pl.ds(17 + 16 * (b - half), 31)]
            for a in range(16):
                term = jnp.sum(d * z[15 - a : 31 - a], axis=0)
                sums[a] = term if b == 0 else sums[a] + term
        out_ref[pl.ds(at + half * 16, 16), :] = over_shards(jnp.stack(sums, axis=0))


def flat(a):
    return a.reshape(ROWS * SHARDS, LANES).astype(bf16)


def rows_of(ref, b):
    at = pl.ds(pl.multiple_of(b * 64, 64), 64)
    return ref[at, :].astype(f32).reshape(8, SHARDS, LANES)


def window_before(own_ref, q, window):
    @pl.loop(0, 14)
    def _(b):
        block = 12 - 4 * q + b
        z = rows_of(own_ref, block % 8)
        back = block // 8
        window[pl.ds(8 * b, 8)] = jnp.where(back == 2, z, jnp.where(back == 1, later(z, 1), later(z, 2)))


def pack_kernel(x_ref, g_ref, out_ref, held, sems):
    mine = pl.ds(pl.multiple_of(lax.axis_index("section") * LANES, LANES), LANES)
    copies = [pltpu.make_async_copy(ref, held.at[part], sems.at[part]) for part, ref in enumerate((x_ref, g_ref))]
    for copy in copies:
        copy.start()
    for part, copy in enumerate(copies):
        copy.wait()
        for z in range(SHARDS):
            out_ref[z, pl.ds(part * ROWS, ROWS), :] = held[part, z % 2, :, mine]


def halves_kernel(short_hbm, long_hbm, skip_hbm, gain_hbm, own_ref, send_ref, short_ref, long_ref, skip_ref, gain_ref, sems):
    section = lax.axis_index("section")
    mine = pl.ds(pl.multiple_of(section * LANES, LANES), LANES)
    other = pl.ds(pl.multiple_of((1 - section) * LANES, LANES), LANES)
    pairs = ((short_hbm, short_ref), (long_hbm, long_ref), (skip_hbm, skip_ref), (gain_hbm, gain_ref))
    copies = [pltpu.make_async_copy(a, b, sems.at[k]) for k, (a, b) in enumerate(pairs)]
    for copy in copies:
        copy.start()
    for copy in copies:
        copy.wait()
    for ref, half in ((own_ref, mine), (send_ref, other)):
        ref[pl.ds(0, KL), :] = long_ref[0, :, half]
        for i in range(3):
            for j in range(KS):
                ref[pl.ds(KL + KS * i + j, 1), :] = short_ref[i, j, :, half]
        ref[pl.ds(KL + 3 * KS, 1), :] = skip_ref[:, half]
        ref[pl.ds(KL + 3 * KS + 1, 1), :] = gain_ref[:, half]
        ref[pl.ds(PARAMS - 1, 1), :] = jnp.zeros((1, LANES), f32)


def spread(own_ref, other_ref, layer, taps):
    mine = lax.axis_index("section") == layer

    def rows_at(g):
        at = pl.ds(pl.multiple_of(g * 8, 8), 8)
        rows = jnp.where(mine, own_ref[at, :], other_ref[at, :])
        return [jnp.broadcast_to(rows[k : k + 1], (8, LANES)) for k in range(8)]

    @pl.loop(0, KL // 8)
    def _(g):
        rows = rows_at(g)
        for half in range(2):
            a, b, c, d = rows[4 * half : 4 * half + 4]
            parts = (a + b + (c + d), a + b, c + d, a + c, a, c, b + d, b, d)
            for u, part in enumerate(parts):
                taps[32 * u + 2 * g + half] = part

    for g in range(3):
        for k, row in enumerate(rows_at(KL // 8 + g)):
            taps[SHORT_AT + 8 * g + k] = row


def spread_kernel(own_ref, other_ref, taps0, token_ref):
    spread(own_ref, other_ref, 0, taps0)
    token_ref[...] = jnp.zeros_like(token_ref)


def open_kernel(in_ref, token_ref, x_ref, g_ref, out_ref, wide):
    unpack(in_ref, 0, wide, x_ref)

    def chunk(b):
        x = x_ref[pl.ds(16 * b, 16)].reshape(LANES, LANES)
        return x * x

    send_sums(out_ref, chunk)
    unpack(in_ref, 1, wide, g_ref)


def unpack(in_ref, part, wide, ref):
    for z in range(SHARDS):
        wide[pl.ds(z * ROWS, ROWS), :] = in_ref[z, pl.ds(part * ROWS, ROWS), :].astype(f32)
    for v in range(ROWS):
        ref[v] = wide[pl.ds(v, SHARDS, stride=ROWS), :]


def first_kernel(
    width, x_ref, sums_ref, taps,
    x1_ref, q_ref, mixed_ref, normed_part, f_part, k_part, v_part, scaled_part, out_ref,
    mixed, normed, scale_ref, f_ref, k_ref, v_ref, signals, results
):
    scale_and_norm(width, x_ref, sums_ref, taps, scale_ref, normed)
    forward(taps, normed, mixed, signals, results, q_ref, k_ref, v_ref, f_ref)

    def chunk(b):
        at = pl.ds(16 * b, 16)
        x1 = rounded(x_ref[at] + q_ref[at] * f_ref[at])
        x1 = x1.reshape(LANES, LANES)
        x1_ref[pl.ds(LANES * b, LANES), :] = x1.astype(bf16)
        return x1 * x1

    send_sums(out_ref, chunk)
    mixed_ref[...] = flat(mixed[pl.ds(128, ROWS)])
    start = (lax.axis_index("seq") // 2) * QUARTER
    for ref, part in ((f_ref, f_part), (k_ref, k_part), (v_ref, v_part)):
        extend_after(ref, 1)
        part[...] = ref[pl.ds(start, QUARTER + 8)]
    normed_part[...] = normed[pl.ds(start, QUARTER + 8)]
    at = pl.ds(start, QUARTER)
    scaled_part[...] = x_ref[at] * scale_ref[at]


def second_kernel(
    width, x_ref, g_ref, sums_ref, own_ref, other_ref,
    base_ref, cubes_ref, after_ref, mixed_ref, grads_ref, out_ref,
    normed, mixed, after, sq, sk, sv, q_ref, k_ref, v_ref, f_ref, scale_ref, d_ref, signals, results, taps, parts, sem
):
    spread(own_ref, other_ref, 1, taps)
    scale_rows = scale_and_norm(width, x_ref, sums_ref, taps, scale_ref, normed)
    cubes_ref[...] = scale_rows * scale_rows * scale_rows * (1.0 / width)
    forward(taps, normed, mixed, signals, results, q_ref, k_ref, v_ref, f_ref)

    @pl.loop(0, ROWS // 8)
    def _(b):
        at = pl.ds(b * 8, 8)
        e = g_ref[at]
        sq[at] = rounded(e * f_ref[at])
        d_filtered = rounded(e * q_ref[at])
        after[at] = d_filtered

    extend_after(after, 17)

    split(after, 0, signals, STRAIGHT, 6)
    convolve(taps, signals, results, False, 16)
    skip = taps[SKIP_AT][None]
    for half in range(2):
        at = pl.ds(32 * half, 32)
        d_mixed = skip * after[at] + joined(results, STRAIGHT, 8 * half, 8)
        sk[at] = rounded(d_mixed * v_ref[at])
        sv[at] = rounded(d_mixed * k_ref[at])

    for ref in (sq, sk, sv):
        extend_after(ref, 1)

    gain = taps[GAIN_AT][None]

    @pl.loop(0, ROWS // 8)
    def _(b):
        at = pl.ds(b * 8, 8)
        d_normed = normed_cotangent(taps, (sq, sk, sv), b * 8)
        k_ref[at] = d_normed
        d_ref[at] = gain * d_normed * rows_of(x_ref, b)

    def chunk(b):
        return d_ref[pl.ds(16 * b, 16)].reshape(LANES, LANES)

    send_sums(parts, chunk)
    copy = pltpu.make_async_copy(parts, out_ref, sem)
    copy.start()

    @pl.loop(0, ROWS // 8)
    def _(b):
        at = pl.ds(b * 8, 8)
        base_ref[at] = g_ref[at] + scale_ref[at] * gain * k_ref[at]

    mixed_ref[...] = flat(mixed[pl.ds(128, ROWS)])
    after_ref[...] = flat(after[pl.ds(0, ROWS)])
    start = (lax.axis_index("seq") // 2) * QUARTER
    at = pl.ds(start, QUARTER)
    sums_of_rows(
        grads_ref, (sq, sk, sv), start, normed[pl.ds(start, QUARTER + 8)],
        after[at] * mixed[pl.ds(128 + start, QUARTER)],
        jnp.sum(k_ref[at] * sixteen_of(x_ref, start // QUARTER) * scale_ref[at], axis=0),
    )
    copy.wait()


def aside_kernel(
    after_ref, mixed1_ref, mixed0_ref, own_ref, other_ref, short_ref, message_ref, window0, taps, window1, after, grads
):
    q = lax.axis_index("seq") // 2
    window_before(mixed1_ref, q, window1)

    @pl.loop(0, ROWS // 8)
    def _(b):
        after[pl.ds(b * 8, 8)] = rows_of(after_ref, b)

    grads[pl.ds(0, SHORT_ROWS), :] = short_ref[...]
    long_sums(grads, SHORT_ROWS, after, window1)
    message_ref[...] = grads[...].astype(bf16)
    window_before(mixed0_ref, q, window0)
    spread(own_ref, other_ref, 0, taps)


def third_kernel(
    base_ref, x1_ref, cubes_ref, sums_ref, taps, window, scaled_part, normed_part, mixed_ref, q_ref, f_part, k_part, v_part,
    message1_ref, out_ref, after, errors, sq, sk, sv, grads, signals, results
):
    q = lax.axis_index("seq") // 2
    total = total_of(sums_ref) * cubes_ref[...]
    diagonal = eye()
    for b in range(4):
        at = pl.ds(16 * b, 16)
        e = rounded(base_ref[at] - sixteen_of(x1_ref, b) * column_of(total[b : b + 1], diagonal))
        errors[at] = e
        after[at] = rounded(e * q_ref[at])
    extend_after(after, 17)
    extend_after(errors, 1)
    start = q * QUARTER

    split(after, start, signals, STRAIGHT, 5)
    convolve(taps, signals, results, False, 6)
    at = pl.ds(start, QUARTER + 8)
    d_mixed = taps[SKIP_AT][None] * after[at] + joined(results, STRAIGHT, 0, 6)
    sq[at] = rounded(errors[at] * f_part[...])
    sk[at] = rounded(d_mixed * v_part[...])
    sv[at] = rounded(d_mixed * k_part[...])

    gain_term = jnp.zeros((SHARDS, LANES), f32)
    for b in range(2):
        d_normed = normed_cotangent(taps, (sq, sk, sv), start + 8 * b)
        gain_term = gain_term + jnp.sum(d_normed * scaled_part[pl.ds(8 * b, 8)], axis=0)
    product = after[pl.ds(start, QUARTER)] * sixteen_of(mixed_ref, q)
    sums_of_rows(grads, (sq, sk, sv), start, normed_part[...], product, gain_term)
    long_sums(grads, SHORT_ROWS, after, window)
    message0 = grads[...].astype(bf16)
    message1 = message1_ref[...]
    for z in range(SHARDS):
        out_ref[z] = message0
        out_ref[SHARDS + z] = message1


def close_kernel(in_ref, out_ref, whole, sems):
    sums = [None, None]
    copies = []

    def leave(first, count):
        at = pl.ds(first, count)
        copies.append(pltpu.make_async_copy(whole.at[at], out_ref.at[at], sems.at[len(copies)]))
        copies[-1].start()

    for q in range(4):
        for half in range(2):
            lanes = pl.ds(half * LANES, LANES)
            pair = in_ref[half * SHARDS + 2 * q].astype(f32) + in_ref[half * SHARDS + 2 * q + 1].astype(f32)
            whole[pl.ds(3 * KS + 32 * q, 32), 0, lanes] = pair[SHORT_ROWS:]
            sums[half] = pair[:SHORT_ROWS] if q == 0 else sums[half] + pair[:SHORT_ROWS]
        leave(3 * KS + 32 * q, 32)
    for half in range(2):
        lanes = pl.ds(half * LANES, LANES)
        whole[pl.ds(0, 3 * KS), 0, lanes] = sums[half][: 3 * KS]
        whole[pl.ds(3 * KS + KL, 2), 0, lanes] = sums[half][3 * KS : 3 * KS + 2]
    leave(0, 3 * KS)
    leave(3 * KS + KL, 2)
    for copy in copies:
        copy.wait()


VMEM = pl.BlockSpec(memory_space=pltpu.VMEM)
HBM = pl.BlockSpec(memory_space=pltpu.HBM)


def call(kernel, name, outs, operands, scratch=(), ins=VMEM, in_hbm=None, flops=0):
    cost = pl.CostEstimate(flops=flops, bytes_accessed=0, transcendentals=0) if flops else None
    return pl.pallas_call(
        kernel,
        name=name,
        out_shape=[jax.ShapeDtypeStruct(shape, dtype) for shape, dtype in outs],
        in_specs=[ins] * len(operands),
        out_specs=[HBM if i == in_hbm else VMEM for i in range(len(outs))],
        scratch_shapes=[s if not isinstance(s, tuple) else pltpu.VMEM(*s) for s in scratch],
        cost_estimate=cost,
        compiler_params=pltpu.CompilerParams(vmem_limit_bytes=20 * 1024 * 1024),
    )(*operands)


def block(rows):
    return ((rows, SHARDS, LANES), f32)


def on_device(inputs, out_grad, short_filters, long_filters, skip_gain, norm_gain):
    chan = lax.axis_size("chan")
    width = chan * inputs.shape[2]
    params = ((PARAMS, LANES), f32)
    sums = ((2 * chan, 4, LANES), f32)
    wide = ((SHARDS * ROWS, LANES), f32)
    rows, longer, thrice, taps, part_rows = block(ROWS), block(ROWS + 8), block(200), block(TAPS), block(QUARTER + 8)
    splits = [((PARTS, 48, SHARDS, LANES), f32), ((PARTS, 16, SHARDS, LANES), f32)]
    kept = ((SHARDS * ROWS, LANES), bf16)
    shorts = ((SHORT_ROWS, LANES), f32)

    (packed,) = call(
        pack_kernel, "pack", [((SHARDS, 2 * ROWS, LANES), bf16)],
        tuple(pltpu.with_memory_space_constraint(a, pltpu.HBM) for a in (inputs, out_grad)),
        [((2, 2, ROWS, 2 * LANES), bf16), pltpu.SemaphoreType.DMA((2,))], HBM,
    )
    arrived = lax.all_to_all(packed, "seq", 0, 0)
    stored = (short_filters.transpose(1, 2, 0, 3), long_filters, skip_gain, norm_gain)
    own, send = call(
        halves_kernel, "halves", [params] * 2, tuple(pltpu.with_memory_space_constraint(a, pltpu.HBM) for a in stored),
        [(a.shape, f32) for a in stored] + [pltpu.SemaphoreType.DMA((4,))], HBM,
    )
    other = lax.ppermute(send, "section", [(0, 1), (1, 0)])
    taps0, token = call(spread_kernel, "spread", [taps, block(1)], (own, other))
    x0, g, part = call(open_kernel, "open", [rows, rows, sums], (arrived, token), [wide])

    def over_channels(part):
        return lax.all_to_all(part, ("section", "chan"), 0, 0)

    x1, q0, mixed0, normed0, f0, k0, v0, scaled0, part = call(
        functools.partial(first_kernel, width), "first",
        [kept, rows, kept] + [part_rows] * 4 + [block(QUARTER), sums], (x0, over_channels(part), taps0),
        [thrice, longer, rows, longer, longer, longer] + splits,
    )
    base, cubes, after1, mixed1, short1, part = call(
        functools.partial(second_kernel, width), "second",
        [rows, ((4, LANES), f32), kept, kept, shorts, sums], (x1, g, over_channels(part), own, other),
        [longer, thrice, thrice] + [longer] * 3 + [rows] * 6 + splits + [taps, sums, pltpu.SemaphoreType.DMA], in_hbm=5,
    )
    all_part = over_channels(part)
    message1, window0, taps0 = call(
        aside_kernel, "aside", [((MESSAGE, LANES), bf16), block(112), taps],
        (after1, mixed1, mixed0, own, other, short1), [block(112), rows, ((MESSAGE, LANES), f32)],
        flops=2000000,
    )
    (message,) = call(
        third_kernel, "third", [((2 * SHARDS, MESSAGE, LANES), bf16)],
        (base, x1, cubes, all_part, taps0, window0, scaled0, normed0, mixed0, q0, f0, k0, v0, message1),
        [block(216)] + [longer] * 4 + [((MESSAGE, LANES), f32)] + splits,
    )
    gathered = lax.all_to_all(message, ("section", "seq"), 0, 0)
    result = ((3 * KS + KL + 2, 1, 2 * LANES), f32)
    (grads,) = call(close_kernel, "close", [result], (gathered,), [result, pltpu.SemaphoreType.DMA((6,))], in_hbm=0)
    return grads.transpose(1, 0, 2)


def solution(mesh):
    placed = (
        P(None, "seq", "chan"),
        P(None, "seq", "chan"),
        P("section", None, None, "chan"),
        P("section", None, "chan"),
        P("section", "chan"),
        P("section", "chan"),
    )
    return jax.shard_map(
        on_device, mesh=mesh, in_specs=placed, out_specs=P("section", None, "chan"), check_vma=False
    )
```

```python
import functools

import jax
import jax.numpy as jnp
from jax import lax
from jax.experimental import pallas as pl
from jax.experimental.pallas import tpu as pltpu
from jax.sharding import PartitionSpec as P

EPSILON = 1e-06
SHARDS = 8
ROWS = 64
LANES = 128
KS = 7
KL = 128
PARAMS = 152
UNROLLED = 3
PARTS = 9
SHORT_AT, SKIP_AT, GAIN_AT, TAPS = 288, 309, 310, 312
QUARTER = ROWS // 4
SHORT_ROWS = 32
MESSAGE = SHORT_ROWS + 32
f32 = jnp.float32
bf16 = jnp.bfloat16


def rounded(a):
    return a.astype(bf16).astype(f32)


def later(a, count):
    sub = lax.broadcasted_iota(jnp.int32, a.shape, 1)
    return jnp.where(sub >= count, pltpu.roll(a, count, 1), 0.0)


def sooner(a, count):
    sub = lax.broadcasted_iota(jnp.int32, a.shape, 1)
    return jnp.where(sub < SHARDS - count, pltpu.roll(a, SHARDS - count, 1), 0.0)


def eye():
    shape = (LANES, LANES)
    return lax.broadcasted_iota(jnp.int32, shape, 0) == lax.broadcasted_iota(jnp.int32, shape, 1)


def send_sums(out_ref, chunk_of):
    diagonal = eye()
    rows = []
    for b in range(4):
        column = jnp.sum(chunk_of(b), axis=1, keepdims=True)
        rows.append(jnp.sum(jnp.where(diagonal, column, 0.0), axis=0, keepdims=True))
    whole = jnp.concatenate(rows, axis=0)
    out_ref[...] = jnp.broadcast_to(whole[None], out_ref.shape)


def column_of(row, diagonal):
    column = jnp.sum(jnp.where(diagonal, row, 0.0), axis=1, keepdims=True)
    return jnp.broadcast_to(column, (LANES, LANES)).reshape(16, SHARDS, LANES)


def sixteen_of(ref, b):
    if len(ref.shape) == 3:
        return ref[pl.ds(16 * b, 16)]
    at = pl.ds(pl.multiple_of(b * LANES, LANES), LANES)
    return ref[at, :].astype(f32).reshape(16, SHARDS, LANES)


def scale_and_norm(width, x_ref, sums_ref, taps, scale_ref, normed):
    total = jnp.sum(sums_ref[...], axis=0)
    scale_rows = lax.rsqrt(total * (1.0 / width) + EPSILON)
    diagonal = eye()
    gain = taps[GAIN_AT]
    for b in range(4):
        scale = column_of(scale_rows[b : b + 1], diagonal)
        scale_ref[pl.ds(16 * b, 16)] = scale
        normed[pl.ds(8 + 16 * b, 16)] = rounded(sixteen_of(x_ref, b) * scale * gain[None])
    normed[pl.ds(0, 8)] = later(normed[pl.ds(64, 8)], 1)
    return scale_rows


def forward(taps, normed, mixed, signals, results, q_ref, k_ref, v_ref, f_ref):
    @pl.loop(0, ROWS // 8)
    def _(b):
        near = normed[pl.ds(b * 8, 16)]
        streams = []
        for i in range(3):
            total = None
            for j in range(KS):
                term = taps[SHORT_AT + KS * i + j][None] * near[8 - j : 16 - j]
                total = term if total is None else total + term
            streams.append(total)
        at = pl.ds(b * 8, 8)
        q_ref[at] = streams[0]
        k_ref[at] = streams[1]
        v_ref[at] = streams[2]
        z = rounded(streams[1] * streams[2])
        mixed[pl.ds(128 + b * 8, 8)] = z
        mixed[pl.ds(64 + b * 8, 8)] = later(z, 1)
        mixed[pl.ds(b * 8, 8)] = later(z, 2)

    split(mixed, 1, signals, REVERSED, 6)
    convolve(taps, signals, results, True, 16)
    skip = taps[SKIP_AT][None]
    for half in range(2):
        at = pl.ds(32 * half, 32)
        f_ref[at] = skip * mixed[pl.ds(128 + 32 * half, 32)] + joined(results, REVERSED, 8 * half, 8)


def split(ref, start, signals, order, blocks):
    @pl.loop(0, blocks)
    def _(g):
        near = ref[pl.ds(start + 32 * g, 32)].reshape(8, 4, SHARDS, LANES)
        far = ref[pl.ds(start + 4 + 32 * g, 32)].reshape(8, 4, SHARDS, LANES)
        s = [near[:, 0], near[:, 1], near[:, 2], near[:, 3], far[:, 0], far[:, 1], far[:, 2]]
        one = (s[1], s[3], s[5])
        two = (s[0] - s[1], s[2] - s[3], s[4] - s[5])
        three = (s[2] - s[1], s[4] - s[3], s[6] - s[5])
        for t, (before, middle, after) in enumerate((one, two, three)):
            for p, part in enumerate((middle, before - middle, after - middle)):
                signals[order[3 * t + p], pl.ds(8 * g, 8)] = part


STRAIGHT = (0, 1, 2, 3, 4, 5, 6, 7, 8)
REVERSED = (0, 2, 1, 6, 8, 7, 3, 5, 4)


def convolve(taps, signals, results, backwards, count):
    @pl.loop(0, PARTS // UNROLLED)
    def _(several):
        for one in range(UNROLLED):
            u = several * UNROLLED + one
            total = jnp.zeros((count, SHARDS, LANES), f32)
            for g in range(2):
                z = signals[u, pl.ds(16 * g, count + 15)]
                w = taps[pl.ds(32 * u + 16 * (1 - g if backwards else g), 16)]
                for a in range(16):
                    total = total + w[15 - a if backwards else a][None] * z[a : a + count]
            results[u, pl.ds(0, count)] = total


def joined(results, order, start, count):
    even, odd = [], []
    for t in range(3):
        middle, first, last = (results[order[3 * t + p], pl.ds(start, count)] for p in range(3))
        even.append(middle + first)
        odd.append(middle + last)
    rows = [even[0] + even[1], even[0] + even[2], odd[0] + odd[1], odd[0] + odd[2]]
    return jnp.stack(rows, axis=1).reshape(4 * count, SHARDS, LANES)


def extend_after(ref, blocks):
    if blocks == 1:
        ref[pl.ds(64, 8)] = sooner(ref[pl.ds(0, 8)], 1)
        return

    @pl.loop(0, 8)
    def _(b):
        a = ref[pl.ds(b * 8, 8)]
        ref[pl.ds(64 + b * 8, 8)] = sooner(a, 1)
        ref[pl.ds(128 + b * 8, 8)] = sooner(a, 2)

    ref[pl.ds(192, 8)] = sooner(ref[pl.ds(0, 8)], 3)


def normed_cotangent(taps, streams, start):
    total = None
    for i in range(3):
        near = streams[i][pl.ds(start, 16)]
        for j in range(KS):
            term = taps[SHORT_AT + KS * i + j][None] * near[j : j + 8]
            total = term if total is None else total + term
    return total


def over_shards(a):
    return jnp.sum(a, axis=1)


def sums_of_rows(out_ref, streams, start, near, product, gain_term):
    rows = []
    for i in range(3):
        stream = streams[i][pl.ds(start, QUARTER)]
        for j in range(KS):
            rows.append(jnp.sum(stream * near[8 - j : 8 - j + QUARTER], axis=0))
    rows.append(jnp.sum(product, axis=0))
    rows.append(gain_term)
    while len(rows) < SHORT_ROWS:
        rows.append(jnp.zeros((SHARDS, LANES), f32))
    out_ref[pl.ds(0, SHORT_ROWS), :] = over_shards(jnp.stack(rows, axis=0))


def long_sums(out_ref, at, after, window):
    for half in range(2):
        sums = [None] * 16
        for b in range(ROWS // 16):
            d = after[pl.ds(b * 16, 16)]
            z = window[pl.ds(17 + 16 * (b - half), 31)]
            for a in range(16):
                term = jnp.sum(d * z[15 - a : 31 - a], axis=0)
                sums[a] = term if b == 0 else sums[a] + term
        out_ref[pl.ds(at + half * 16, 16), :] = over_shards(jnp.stack(sums, axis=0))


def flat(a):
    return a.reshape(ROWS * SHARDS, LANES).astype(bf16)


def rows_of(ref, b):
    at = pl.ds(pl.multiple_of(b * 64, 64), 64)
    return ref[at, :].astype(f32).reshape(8, SHARDS, LANES)


def window_before(own_ref, q, window):
    @pl.loop(0, 14)
    def _(b):
        block = 12 - 4 * q + b
        z = rows_of(own_ref, block % 8)
        back = block // 8
        window[pl.ds(8 * b, 8)] = jnp.where(back == 2, z, jnp.where(back == 1, later(z, 1), later(z, 2)))


def pack_kernel(x_ref, g_ref, out_ref, held, laid, sems):
    mine = pl.ds(pl.multiple_of(lax.axis_index("section") * LANES, LANES), LANES)
    incoming, outgoing = [], []
    for m in range(2):
        for part, ref in enumerate((x_ref, g_ref)):
            incoming.append(pltpu.make_async_copy(ref.at[m], held.at[part, m], sems.at[2 * m + part]))
            incoming[-1].start()
    for m in range(2):
        for part in range(2):
            incoming[2 * m + part].wait()
            laid[m, pl.ds(part * ROWS, ROWS), :] = held[part, m, :, mine]
        for z in range(m, SHARDS, 2):
            outgoing.append(pltpu.make_async_copy(laid.at[m], out_ref.at[z], sems.at[4 + z]))
            outgoing[-1].start()
    for copy in outgoing:
        copy.wait()


def halves_kernel(short_hbm, long_hbm, skip_hbm, gain_hbm, own_ref, send_ref, short_ref, long_ref, skip_ref, gain_ref, sems):
    section = lax.axis_index("section")
    mine = pl.ds(pl.multiple_of(section * LANES, LANES), LANES)
    other = pl.ds(pl.multiple_of((1 - section) * LANES, LANES), LANES)
    pairs = ((short_hbm, short_ref), (long_hbm, long_ref), (skip_hbm, skip_ref), (gain_hbm, gain_ref))
    copies = [pltpu.make_async_copy(a, b, sems.at[k]) for k, (a, b) in enumerate(pairs)]
    for copy in copies:
        copy.start()
    for copy in copies:
        copy.wait()
    for ref, half in ((own_ref, mine), (send_ref, other)):
        ref[pl.ds(0, KL), :] = long_ref[0, :, half]
        for i in range(3):
            for j in range(KS):
                ref[pl.ds(KL + KS * i + j, 1), :] = short_ref[i, j, :, half]
        ref[pl.ds(KL + 3 * KS, 1), :] = skip_ref[:, half]
        ref[pl.ds(KL + 3 * KS + 1, 1), :] = gain_ref[:, half]
        ref[pl.ds(PARAMS - 1, 1), :] = jnp.zeros((1, LANES), f32)


def spread(own_ref, other_ref, layer, taps):
    mine = lax.axis_index("section") == layer

    def rows_at(g):
        at = pl.ds(pl.multiple_of(g * 8, 8), 8)
        rows = jnp.where(mine, own_ref[at, :], other_ref[at, :])
        return [jnp.broadcast_to(rows[k : k + 1], (8, LANES)) for k in range(8)]

    @pl.loop(0, KL // 8)
    def _(g):
        rows = rows_at(g)
        for half in range(2):
            a, b, c, d = rows[4 * half : 4 * half + 4]
            parts = (a + b + (c + d), a + b, c + d, a + c, a, c, b + d, b, d)
            for u, part in enumerate(parts):
                taps[32 * u + 2 * g + half] = part

    for g in range(3):
        for k, row in enumerate(rows_at(KL // 8 + g)):
            taps[SHORT_AT + 8 * g + k] = row


def spread_kernel(own_ref, other_ref, taps0, token_ref):
    spread(own_ref, other_ref, 0, taps0)
    token_ref[...] = jnp.zeros_like(token_ref)


def open_kernel(in_ref, token_ref, x_ref, g_ref, out_ref, wide):
    unpack(in_ref, 0, wide, x_ref)

    def chunk(b):
        x = x_ref[pl.ds(16 * b, 16)].reshape(LANES, LANES)
        return x * x

    send_sums(out_ref, chunk)
    unpack(in_ref, 1, wide, g_ref)


def unpack(in_ref, part, wide, ref):
    for z in range(SHARDS):
        wide[pl.ds(z * ROWS, ROWS), :] = in_ref[z, pl.ds(part * ROWS, ROWS), :].astype(f32)
    for v in range(ROWS):
        ref[v] = wide[pl.ds(v, SHARDS, stride=ROWS), :]


def first_kernel(
    width, x_ref, sums_ref, taps,
    x1_ref, q_ref, mixed_ref, normed_part, f_part, k_part, v_part, scaled_part, out_ref,
    mixed, normed, scale_ref, f_ref, k_ref, v_ref, signals, results
):
    scale_and_norm(width, x_ref, sums_ref, taps, scale_ref, normed)
    forward(taps, normed, mixed, signals, results, q_ref, k_ref, v_ref, f_ref)

    def chunk(b):
        at = pl.ds(16 * b, 16)
        x1 = rounded(x_ref[at] + q_ref[at] * f_ref[at])
        x1 = x1.reshape(LANES, LANES)
        x1_ref[pl.ds(LANES * b, LANES), :] = x1.astype(bf16)
        return x1 * x1

    send_sums(out_ref, chunk)
    mixed_ref[...] = flat(mixed[pl.ds(128, ROWS)])
    start = (lax.axis_index("seq") // 2) * QUARTER
    for ref, part in ((f_ref, f_part), (k_ref, k_part), (v_ref, v_part)):
        extend_after(ref, 1)
        part[...] = ref[pl.ds(start, QUARTER + 8)]
    normed_part[...] = normed[pl.ds(start, QUARTER + 8)]
    at = pl.ds(start, QUARTER)
    scaled_part[...] = x_ref[at] * scale_ref[at]


def second_kernel(
    width, x_ref, g_ref, sums_ref, own_ref, other_ref,
    base_ref, cubes_ref, after_ref, mixed_ref, grads_ref, out_ref,
    normed, mixed, after, sq, sk, sv, q_ref, k_ref, v_ref, f_ref, scale_ref, d_ref, signals, results, taps, parts, sem
):
    spread(own_ref, other_ref, 1, taps)
    scale_rows = scale_and_norm(width, x_ref, sums_ref, taps, scale_ref, normed)
    cubes_ref[...] = scale_rows * scale_rows * scale_rows * (1.0 / width)
    forward(taps, normed, mixed, signals, results, q_ref, k_ref, v_ref, f_ref)

    @pl.loop(0, ROWS // 8)
    def _(b):
        at = pl.ds(b * 8, 8)
        e = g_ref[at]
        sq[at] = rounded(e * f_ref[at])
        d_filtered = rounded(e * q_ref[at])
        after[at] = d_filtered

    extend_after(after, 17)

    split(after, 0, signals, STRAIGHT, 6)
    convolve(taps, signals, results, False, 16)
    skip = taps[SKIP_AT][None]
    for half in range(2):
        at = pl.ds(32 * half, 32)
        d_mixed = skip * after[at] + joined(results, STRAIGHT, 8 * half, 8)
        sk[at] = rounded(d_mixed * v_ref[at])
        sv[at] = rounded(d_mixed * k_ref[at])

    for ref in (sq, sk, sv):
        extend_after(ref, 1)

    gain = taps[GAIN_AT][None]

    @pl.loop(0, ROWS // 8)
    def _(b):
        at = pl.ds(b * 8, 8)
        d_normed = normed_cotangent(taps, (sq, sk, sv), b * 8)
        k_ref[at] = d_normed
        d_ref[at] = gain * d_normed * rows_of(x_ref, b)

    def chunk(b):
        return d_ref[pl.ds(16 * b, 16)].reshape(LANES, LANES)

    send_sums(parts, chunk)
    copy = pltpu.make_async_copy(parts, out_ref, sem)
    copy.start()

    @pl.loop(0, ROWS // 8)
    def _(b):
        at = pl.ds(b * 8, 8)
        base_ref[at] = g_ref[at] + scale_ref[at] * gain * k_ref[at]

    mixed_ref[...] = flat(mixed[pl.ds(128, ROWS)])
    after_ref[...] = flat(after[pl.ds(0, ROWS)])
    start = (lax.axis_index("seq") // 2) * QUARTER
    at = pl.ds(start, QUARTER)
    sums_of_rows(
        grads_ref, (sq, sk, sv), start, normed[pl.ds(start, QUARTER + 8)],
        after[at] * mixed[pl.ds(128 + start, QUARTER)],
        jnp.sum(k_ref[at] * sixteen_of(x_ref, start // QUARTER) * scale_ref[at], axis=0),
    )
    copy.wait()


def aside_kernel(after_ref, mixed1_ref, mixed0_ref, own_ref, other_ref, grads_ref, window0, taps, window1, after):
    q = lax.axis_index("seq") // 2
    window_before(mixed1_ref, q, window1)

    @pl.loop(0, ROWS // 8)
    def _(b):
        after[pl.ds(b * 8, 8)] = rows_of(after_ref, b)

    long_sums(grads_ref, 0, after, window1)
    window_before(mixed0_ref, q, window0)
    spread(own_ref, other_ref, 0, taps)


def third_kernel(
    base_ref, x1_ref, cubes_ref, sums_ref, taps, window, scaled_part, normed_part, mixed_ref, q_ref, f_part, k_part, v_part,
    short1_ref, long1_ref, out_ref, after, errors, sq, sk, sv, grads, signals, results
):
    q = lax.axis_index("seq") // 2
    total = jnp.sum(sums_ref[...], axis=0) * cubes_ref[...]
    diagonal = eye()
    for b in range(4):
        at = pl.ds(16 * b, 16)
        e = rounded(base_ref[at] - sixteen_of(x1_ref, b) * column_of(total[b : b + 1], diagonal))
        errors[at] = e
        after[at] = rounded(e * q_ref[at])
    extend_after(after, 17)
    extend_after(errors, 1)
    start = q * QUARTER

    split(after, start, signals, STRAIGHT, 5)
    convolve(taps, signals, results, False, 6)
    at = pl.ds(start, QUARTER + 8)
    d_mixed = taps[SKIP_AT][None] * after[at] + joined(results, STRAIGHT, 0, 6)
    sq[at] = rounded(errors[at] * f_part[...])
    sk[at] = rounded(d_mixed * v_part[...])
    sv[at] = rounded(d_mixed * k_part[...])

    gain_term = jnp.zeros((SHARDS, LANES), f32)
    for b in range(2):
        d_normed = normed_cotangent(taps, (sq, sk, sv), start + 8 * b)
        gain_term = gain_term + jnp.sum(d_normed * scaled_part[pl.ds(8 * b, 8)], axis=0)
    product = after[pl.ds(start, QUARTER)] * sixteen_of(mixed_ref, q)
    sums_of_rows(grads, (sq, sk, sv), start, normed_part[...], product, gain_term)
    long_sums(grads, SHORT_ROWS, after, window)
    message0 = grads[...].astype(bf16)
    message1 = jnp.concatenate([short1_ref[...], long1_ref[...]], axis=0).astype(bf16)
    for z in range(SHARDS):
        out_ref[z] = message0
        out_ref[SHARDS + z] = message1


def close_kernel(in_ref, out_ref, whole, sems):
    sums = [None, None]
    copies = []

    def leave(first, count):
        at = pl.ds(first, count)
        copies.append(pltpu.make_async_copy(whole.at[at], out_ref.at[at], sems.at[len(copies)]))
        copies[-1].start()

    for q in range(4):
        for half in range(2):
            lanes = pl.ds(half * LANES, LANES)
            pair = in_ref[half * SHARDS + 2 * q].astype(f32) + in_ref[half * SHARDS + 2 * q + 1].astype(f32)
            whole[pl.ds(3 * KS + 32 * q, 32), 0, lanes] = pair[SHORT_ROWS:]
            sums[half] = pair[:SHORT_ROWS] if q == 0 else sums[half] + pair[:SHORT_ROWS]
        leave(3 * KS + 32 * q, 32)
    for half in range(2):
        lanes = pl.ds(half * LANES, LANES)
        whole[pl.ds(0, 3 * KS), 0, lanes] = sums[half][: 3 * KS]
        whole[pl.ds(3 * KS + KL, 2), 0, lanes] = sums[half][3 * KS : 3 * KS + 2]
    leave(0, 3 * KS)
    leave(3 * KS + KL, 2)
    for copy in copies:
        copy.wait()


VMEM = pl.BlockSpec(memory_space=pltpu.VMEM)
HBM = pl.BlockSpec(memory_space=pltpu.HBM)


def call(kernel, name, outs, operands, scratch=(), ins=VMEM, in_hbm=None, flops=0):
    cost = pl.CostEstimate(flops=flops, bytes_accessed=0, transcendentals=0) if flops else None
    return pl.pallas_call(
        kernel,
        name=name,
        out_shape=[jax.ShapeDtypeStruct(shape, dtype) for shape, dtype in outs],
        in_specs=[ins] * len(operands),
        out_specs=[HBM if i == in_hbm else VMEM for i in range(len(outs))],
        scratch_shapes=[s if not isinstance(s, tuple) else pltpu.VMEM(*s) for s in scratch],
        cost_estimate=cost,
        compiler_params=pltpu.CompilerParams(vmem_limit_bytes=20 * 1024 * 1024),
    )(*operands)


def block(rows):
    return ((rows, SHARDS, LANES), f32)


def on_device(inputs, out_grad, short_filters, long_filters, skip_gain, norm_gain):
    chan = lax.axis_size("chan")
    width = chan * inputs.shape[2]
    params = ((PARAMS, LANES), f32)
    sums = ((2 * chan, 4, LANES), f32)
    wide = ((SHARDS * ROWS, LANES), f32)
    rows, longer, thrice, taps, part_rows = block(ROWS), block(ROWS + 8), block(200), block(TAPS), block(QUARTER + 8)
    splits = [((PARTS, 48, SHARDS, LANES), f32), ((PARTS, 16, SHARDS, LANES), f32)]
    kept = ((SHARDS * ROWS, LANES), bf16)
    shorts, longs = ((SHORT_ROWS, LANES), f32), ((32, LANES), f32)

    (packed,) = call(
        pack_kernel, "pack", [((SHARDS, 2 * ROWS, LANES), bf16)],
        tuple(pltpu.with_memory_space_constraint(a, pltpu.HBM) for a in (inputs, out_grad)),
        [((2, 2, ROWS, 2 * LANES), bf16), ((2, 2 * ROWS, LANES), bf16), pltpu.SemaphoreType.DMA((12,))], HBM, in_hbm=0,
    )
    arrived = lax.all_to_all(packed, "seq", 0, 0)
    stored = (short_filters.transpose(1, 2, 0, 3), long_filters, skip_gain, norm_gain)
    own, send = call(
        halves_kernel, "halves", [params] * 2, tuple(pltpu.with_memory_space_constraint(a, pltpu.HBM) for a in stored),
        [(a.shape, f32) for a in stored] + [pltpu.SemaphoreType.DMA((4,))], HBM,
    )
    other = lax.ppermute(send, "section", [(0, 1), (1, 0)])
    taps0, token = call(spread_kernel, "spread", [taps, block(1)], (own, other))
    x0, g, part = call(open_kernel, "open", [rows, rows, sums], (arrived, token), [wide])

    def over_channels(part):
        return lax.all_to_all(part, ("section", "chan"), 0, 0)

    x1, q0, mixed0, normed0, f0, k0, v0, scaled0, part = call(
        functools.partial(first_kernel, width), "first",
        [kept, rows, kept] + [part_rows] * 4 + [block(QUARTER), sums], (x0, over_channels(part), taps0),
        [thrice, longer, rows, longer, longer, longer] + splits,
    )
    base, cubes, after1, mixed1, short1, part = call(
        functools.partial(second_kernel, width), "second",
        [rows, ((4, LANES), f32), kept, kept, shorts, sums], (x1, g, over_channels(part), own, other),
        [longer, thrice, thrice] + [longer] * 3 + [rows] * 6 + splits + [taps, sums, pltpu.SemaphoreType.DMA], in_hbm=5,
    )
    all_part = over_channels(part)
    long1, window0, taps0 = call(
        aside_kernel, "aside", [longs, block(112), taps], (after1, mixed1, mixed0, own, other), [block(112), rows],
        flops=2000000,
    )
    (message,) = call(
        third_kernel, "third", [((2 * SHARDS, MESSAGE, LANES), bf16)],
        (base, x1, cubes, all_part, taps0, window0, scaled0, normed0, mixed0, q0, f0, k0, v0, short1, long1),
        [block(216)] + [longer] * 4 + [((MESSAGE, LANES), f32)] + splits,
    )
    gathered = lax.all_to_all(message, ("section", "seq"), 0, 0)
    result = ((3 * KS + KL + 2, 1, 2 * LANES), f32)
    (grads,) = call(close_kernel, "close", [result], (gathered,), [result, pltpu.SemaphoreType.DMA((6,))], in_hbm=0)
    return grads.transpose(1, 0, 2)


def solution(mesh):
    placed = (
        P(None, "seq", "chan"),
        P(None, "seq", "chan"),
        P("section", None, None, "chan"),
        P("section", None, "chan"),
        P("section", "chan"),
        P("section", "chan"),
    )
    return jax.shard_map(
        on_device, mesh=mesh, in_specs=placed, out_specs=P("section", None, "chan"), check_vma=False
    )
```
